256 devices in a mesh: tok: 64 (over y, z, core), feat: 4 (over x).
Axes of the slice: x: 4, y: 4, z: 8, core: 2. Of those that a mesh axis runs over, the one named last changes fastest.
Arguments:
- activations: bfloat16 [16384, 16384], P('tok', 'feat'), may hold values from -0.0625 to 0.0625
- targets: float32 [16384, 32], P('tok'), may hold values from -6 to 6
- counts: int32 [64], P('tok'), may hold values from 1 to 256, 8192 in all
- ridge: float32 [32], replicated, may hold values from 0.1 to 1
Outputs:
- weights: float32 [16384, 32], P('feat')
- residual: float32 [16384, 32], P('tok')
The draws below stay inside these ranges and needn't reach their ends.
Inputs may be any that keep to these rules, and one draw needn't show every extreme that they name: The counts of all shards sum to 8192.
All inputs are finite; a program needn't handle non-finite values.
Results may differ from the reference program's by a relative error of at most 0.033.
Values may be sent and summed in bfloat16 or wider, within the bound.
A program may use at most 64 MiB of HBM per device.

```python
import math
import jax
import jax.numpy as jnp
import numpy as np

D = 16384
K = 32
ROWS_DEV = 256
ITERS = 4
SHARDS = 64
TOKENS = 16384


def steps_of(stream_key, shape, pieces, low, top_value):
    level = 1.0
    for axis_at, blocks in pieces:
        heights = jax.random.uniform(jax.random.fold_in(jax.random.fold_in(stream_key, 6), axis_at), (blocks,), jnp.float32, low / len(pieces), top_value / len(pieces))
        level = level * jnp.repeat(jnp.exp(heights), shape[axis_at] // blocks).reshape((-1,) + (1,) * (len(shape) - 1 - axis_at))
    return level


def split_up(number_of, total, limit, lean):
    portions = [(1 << 20) // math.isqrt(rank ** lean) + 1 for rank in range(2, number_of + 1)]
    surplus, given = total - limit - (number_of - 1), [1] * (number_of - 1)
    while surplus > 0:
        free = [i for i in range(number_of - 1) if given[i] < limit]
        pool, left = sum([portions[i] for i in free]), surplus
        for i in free:
            addition = min(limit - given[i], max(1, left * portions[i] // pool), surplus)
            given[i] = given[i] + addition
            surplus = surplus - addition
    return np.array([limit] + given)


def ragged_sizes(rng, amount, total, limit, slope):
    if amount == 2:
        one = jax.random.randint(rng, (), max(1, total - limit), min(limit, total - 1) + 1)
        return jnp.stack([one, total - one])
    lengths = jnp.asarray(split_up(amount, total, limit, slope), jnp.int32)
    couples = (amount - 1) // 2
    donor, sink = lengths[1:1 + 2 * couples:2], lengths[2:2 + 2 * couples:2]
    room = jnp.minimum(donor - 1, limit - sink)
    shifted = jax.random.randint(jax.random.fold_in(rng, 1), (couples,), 0, 1 << 20) % (room + 1)
    lengths = lengths.at[1:1 + 2 * couples:2].set(donor - shifted).at[2:2 + 2 * couples:2].set(sink + shifted)
    return lengths[jax.random.permutation(jax.random.fold_in(rng, 2), amount)]


def noise(own_key, dims, scale, bound, shards=(), kind=jnp.bfloat16):
    level = steps_of(own_key, dims, shards, -0.22, 0.18) if shards else 1.0
    result = jax.random.normal(own_key, dims, jnp.float32) * scale * level
    return jnp.minimum(jnp.maximum(result, -bound), bound).astype(kind)


def setup_inputs(seed: int = 0) -> dict:
    seeds = jax.random.split(jax.random.key(seed), 5)
    return {
        "activations": noise(seeds[0], (TOKENS, D), (TOKENS // 2) ** -0.5, 0.0625, ((0, 64), (1, 4))),
        "targets": noise(seeds[1], (TOKENS, K), 1.0, 6.0, ((0, 64),), jnp.float32),
        "counts": ragged_sizes(seeds[2], SHARDS, SHARDS * ROWS_DEV // 2, ROWS_DEV, 2).astype(jnp.int32),
        "ridge": jnp.clip(jnp.exp(jax.random.uniform(seeds[3], (K,), jnp.float32, math.log(0.1), math.log(1.0))), 0.1, 1.0),
    }


def gradient_of(activations, resid, weights, ridge):
    summed = jnp.dot(activations.T, resid.astype(jnp.bfloat16), preferred_element_type=jnp.float32)
    grad = summed - ridge[None, :] * weights
    return grad, jnp.sum(grad * grad, axis=0)


def reference(activations, targets, counts, ridge):
    position = jnp.arange(TOKENS, dtype=jnp.int32)
    shard = position // ROWS_DEV
    within = position % ROWS_DEV
    live = (within < counts[shard]).astype(jnp.float32)[:, None]
    residual = targets * live
    weights = jnp.zeros((D, K), jnp.float32)
    grad, gamma = gradient_of(activations, residual, weights, ridge)
    direction = grad
    for step in range(ITERS):
        direct_bf = direction.astype(jnp.bfloat16)
        image = jnp.dot(activations, direct_bf, preferred_element_type=jnp.float32) * live
        delta = jnp.sum(image * image, axis=0) + ridge * jnp.sum(direction * direction, axis=0)
        alpha = gamma / delta
        weights = weights + alpha[None, :] * direction
        residual = residual - alpha[None, :] * image
        if step + 1 < ITERS:
            grad, gamma_new = gradient_of(activations, residual, weights, ridge)
            direction = grad + (gamma_new / gamma)[None, :] * direction
            gamma = gamma_new
    return weights, residual
```

```python
import jax
import jax.numpy as jnp
from jax import lax
from jax.experimental import pallas as pl
from jax.experimental.pallas import tpu as pltpu
from jax.sharding import PartitionSpec as P

ITERS = 4
NY, NZ, NX = 4, 8, 4
CHIPS = NY * NZ
MESH = pl.DeviceIdType.MESH
F32, BF16 = jnp.float32, jnp.bfloat16


def hops(offset):
    dy, dz = offset
    return min(dy, NY - dy) + min(dz, NZ - dz)


OFFSETS = sorted(((dy, dz) for dy in range(NY) for dz in range(NZ)), key=lambda o: (-hops(o), o))
PEERS = CHIPS - 1
GROUPS = ((0, 5), (5, 12), (12, 20), (20, 32))
TILE = 128


def kernel(a_hbm, y_ref, count_ref, ridge_ref, w_out, p_out, r_out, q_out, alpha_out,
           a, ysend, yrecv, mask, r, q, s, p, w, total, tsend, trecv, drow, g, xbuf, xrow, alpha_buf,
           load_sem, push_send, push_recv, y_sems, t_send, t_recv, d_send, d_recv,
           g_send, g_recv, x_send, x_recv, xr_send, xr_recv, pub_local, pub_send, pub_recv):
    tok, x = lax.axis_index("tok"), lax.axis_index("feat")
    core = lax.rem(tok, 2)
    z, y = lax.rem(tok // 2, NZ), tok // (2 * NZ)
    chips = [lax.rem(y + dy, NY) * NZ + lax.rem(z + dz, NZ) for dy, dz in OFFSETS]
    me = chips[-1]
    mine = pl.ds(pl.multiple_of(core * 256, 256), 256)
    others = pl.ds(pl.multiple_of((1 - core) * 256, 256), 256)
    sibling = (me * 2 + 1 - core, x)
    peers = [(chip * 2 + core, x) for chip in chips[:PEERS]]
    x_peers = [(tok, lax.rem(x + d, NX)) for d in (2, 1, 3)]

    def tile(chip):
        return pl.ds(pl.multiple_of(chip * TILE, TILE), TILE)

    def slots(lo, hi):
        return slice(lo * TILE, hi * TILE)

    def send(src, dst, send_sem, recv_sem, device):
        copy = pltpu.make_async_remote_copy(
            src_ref=src, dst_ref=dst, send_sem=send_sem, recv_sem=recv_sem,
            device_id=device, device_id_type=MESH)
        copy.start()
        return copy

    def wait(ref, sem):
        pltpu.make_async_copy(ref, ref, sem).wait()

    for group, (lo, hi) in enumerate(GROUPS):
        for j in range(lo, hi):
            pltpu.make_async_copy(
                a_hbm.at[:, tile(chips[j])], a.at[mine, slots(j, j + 1)], load_sem.at[group]).start()

    barrier = pltpu.get_barrier_semaphore()
    for device in peers + x_peers + [sibling]:
        pl.semaphore_signal(barrier, inc=1, device_id=device, device_id_type=MESH)

    live = (lax.broadcasted_iota(jnp.int32, (32, 256), 1) < count_ref[0]).astype(F32)
    own_rows = pl.ds(pl.multiple_of(core * 16, 16), 16)
    sibling_rows = pl.ds(pl.multiple_of((1 - core) * 16, 16), 16)
    ysend[0:16, :] = y_ref[sibling_rows, :] * live[0:16]
    ysend[16:24, :] = live[0:8]
    r[:, mine] = y_ref[own_rows, :] * live[0:16]
    mask[:, mine] = live[0:8]
    q[...] = jnp.zeros_like(q)
    p[...] = jnp.zeros_like(p)
    w[...] = jnp.zeros_like(w)
    total[...] = jnp.zeros_like(total)

    lane = lax.broadcasted_iota(jnp.int32, (16, TILE), 1)
    sub = lax.broadcasted_iota(jnp.int32, (16, TILE), 0)
    eye = (lane == sub).astype(F32)
    eye2 = (lane == sub + 16).astype(F32)
    pick = (lax.broadcasted_iota(jnp.int32, (16, 32), 1)
            == lax.broadcasted_iota(jnp.int32, (16, 32), 0) + core * 16).astype(F32)
    ridge = jnp.sum(ridge_ref[...] * pick, axis=1, keepdims=True)

    def to_row(column, which):
        return jnp.sum(column * which, axis=0, keepdims=True)

    def to_column(row, which):
        return jnp.sum(row * which, axis=1, keepdims=True)

    def lanes(v):
        out = v[:, 0:TILE]
        for j in range(1, v.shape[1] // TILE):
            out = out + v[:, j * TILE:(j + 1) * TILE]
        return jnp.sum(out, axis=1, keepdims=True)

    def curvature(n):
        wait(drow.at[n, pl.ds(0, PEERS)], d_recv.at[n])
        row = drow[n, 0]
        for j in range(1, CHIPS):
            row = row + drow[n, j]
        return to_column(row, eye)

    def send_row(n, j):
        send(drow.at[n, me], drow.at[n, me], d_send, d_recv.at[n], peers[j])

    pl.semaphore_wait(barrier, PEERS + NX)

    y_copy = send(ysend, yrecv, y_sems.at[0], y_sems.at[1], sibling)
    pushes = []
    for group, (lo, hi) in enumerate(GROUPS):
        wait(a.at[mine, slots(lo, hi)], load_sem.at[group])
        part = a.at[mine, slots(lo, hi)]
        pushes.append(send(part, part, push_send.at[group], push_recv.at[group], sibling))
    y_copy.wait()
    r[:, others] = yrecv[0:16, :]
    mask[:, others] = yrecv[16:24, :]
    s[...] = r[...].astype(BF16)
    drow[0, me] = to_row(lanes(r[...] * r[...]), eye)

    def step(n, carry):
        gamma, norm, guess, beta = carry
        for group, (lo, hi) in enumerate(GROUPS):
            @pl.when(n == 0)
            def _():
                pushes[group].wait_recv()
            part = jnp.dot(s[...], a[:, slots(lo, hi)], preferred_element_type=F32)
            tsend[n, :, slots(lo, hi)] = part.astype(BF16)
            for j in range(lo, min(hi, PEERS)):
                send(tsend.at[n, :, slots(j, j + 1)], trecv.at[n, j], t_send, t_recv.at[n, group], peers[j])
                send_row(n, j)
            if hi == CHIPS:
                summed = part[:, (PEERS - lo) * TILE:]

        @pl.when(n > 0)
        def _():
            p[...] = g[n - 1].astype(F32) + beta * p[...]

        for group, (lo, hi) in reversed(list(enumerate(GROUPS))):
            hi = min(hi, PEERS)
            wait(trecv.at[n, pl.ds(lo, hi - lo)], t_recv.at[n, group])
            for j in range(lo, hi):
                summed = summed + trecv[n, j].astype(F32)
        energy = curvature(n)
        first = n == 0
        alpha = jnp.where(first, 0.0, gamma / (energy + ridge * norm))
        ratio = jnp.where(first, 1.0, alpha / guess)
        fresh = (1.0 - ratio) * total[...] + ratio * summed
        total[...] = fresh
        g[n, :, tile(me)] = (fresh - ridge * (w[:, tile(me)] + alpha * p[:, tile(me)])).astype(BF16)
        for group, (lo, hi) in enumerate(GROUPS):
            for j in range(lo, min(hi, PEERS)):
                part = g.at[n, :, tile(me)]
                send(part, part, g_send, g_recv.at[n, group], peers[j])
        r[...] = r[...] - alpha * q[...]
        w[...] = w[...] + alpha * p[...]

        image = jnp.zeros((16, 512), F32)
        for group, (lo, hi) in reversed(list(enumerate(GROUPS))):
            wait(g.at[n, :, slots(0, min(hi, PEERS) - lo)], g_recv.at[n, group])
            for j in reversed(range(lo, hi)):
                image = image + lax.dot_general(
                    g[n, :, tile(chips[j])], a[:, slots(j, j + 1)], (((1,), (1,)), ((), ())),
                    preferred_element_type=F32)
        xbuf[n, x] = image.astype(BF16)
        for device in x_peers:
            send(xbuf.at[n, x], xbuf.at[n, x], x_send, x_recv.at[n], device)
        grad = g[n].astype(F32)
        xrow[n, x] = to_row(lanes(grad * grad), eye) + to_row(lanes(grad * p[...]), eye2)
        for device in x_peers:
            send(xrow.at[n, x], xrow.at[n, x], xr_send, xr_recv.at[n], device)
        wait(xrow.at[n, pl.ds(0, NX - 1)], xr_recv.at[n])
        row = (xrow[n, 0] + xrow[n, 1]) + (xrow[n, 2] + xrow[n, 3])
        gamma_new = to_column(row, eye)
        cross = to_column(row, eye2)
        beta = jnp.where(first, 0.0, gamma_new / gamma)
        norm = gamma_new + 2.0 * beta * cross + beta * beta * norm
        guess = jnp.where(first, (2.0 / 3.0) * energy / gamma_new, 1.15 * alpha)
        wait(xbuf.at[n, pl.ds(0, NX - 1)], x_recv.at[n])
        image = ((xbuf[n, 0].astype(F32) + xbuf[n, 1].astype(F32))
                 + (xbuf[n, 2].astype(F32) + xbuf[n, 3].astype(F32)))
        fresh_q = image * mask[0:1, :] + beta * q[...]
        q[...] = fresh_q
        s[...] = (r[...] - guess * fresh_q).astype(BF16)
        drow[n + 1, me] = to_row(lanes(fresh_q * fresh_q), eye)
        return gamma_new, norm, guess, beta

    one = jnp.ones((16, 1), F32)
    gamma, norm, guess, beta = lax.fori_loop(0, ITERS, step, (one, one, one, one))

    for j in range(PEERS):
        send_row(ITERS, j)

    def publish(k, here, there, out):
        pltpu.make_async_copy(here, out.at[own_rows], pub_local.at[k]).start()
        send(there, out.at[own_rows], pub_send.at[k], pub_recv.at[k], sibling)

    publish(0, w, w, w_out)
    publish(1, r.at[:, mine], r.at[:, others], r_out)
    publish(2, q.at[:, mine], q.at[:, others], q_out)
    p[...] = g[ITERS - 1].astype(F32) + beta * p[...]
    publish(3, p, p, p_out)
    alpha = gamma / (curvature(ITERS) + ridge * norm)
    alpha_buf[...] = jnp.broadcast_to(alpha, alpha_buf.shape)
    publish(4, alpha_buf, alpha_buf, alpha_out)
    for k, (src, out) in enumerate(((w, w_out), (r.at[:, mine], r_out), (q.at[:, mine], q_out),
                                    (p, p_out), (alpha_buf, alpha_out))):
        wait(src, pub_local.at[k])
        wait(src, pub_send.at[k])
        wait(out.at[sibling_rows], pub_recv.at[k])
    for push in pushes:
        push.wait_send()
    wait(tsend.at[:, :, slots(0, PEERS)], t_send)
    wait(g.at[:, :, slots(0, PEERS)], g_send)
    wait(drow.at[:, pl.ds(0, PEERS)], d_send)
    wait(xbuf.at[:, pl.ds(0, NX - 1)], x_send)
    wait(xrow.at[:, pl.ds(0, NX - 1)], xr_send)


def local(activations, targets, counts, ridge):
    any_ = pl.BlockSpec(memory_space=pl.ANY)
    vmem = pl.BlockSpec(memory_space=pltpu.VMEM)
    dma = pltpu.SemaphoreType.DMA
    groups = len(GROUPS)
    w, p, r, q, alpha = pl.pallas_call(
        kernel,
        out_shape=[jax.ShapeDtypeStruct((32, n), F32) for n in (4096, 4096, 256, 256, TILE)],
        in_specs=[any_, vmem, pl.BlockSpec(memory_space=pltpu.SMEM), vmem],
        out_specs=[any_] * 5,
        scratch_shapes=[
            pltpu.VMEM((512, 4096), BF16),
            pltpu.VMEM((24, 256), F32),
            pltpu.VMEM((24, 256), F32),
            pltpu.VMEM((8, 512), F32),
            pltpu.VMEM((16, 512), F32),
            pltpu.VMEM((16, 512), F32),
            pltpu.VMEM((16, 512), BF16),
            pltpu.VMEM((16, 4096), F32),
            pltpu.VMEM((16, 4096), F32),
            pltpu.VMEM((16, TILE), F32),
            pltpu.VMEM((ITERS, 16, 4096), BF16),
            pltpu.VMEM((ITERS, PEERS, 16, TILE), BF16),
            pltpu.VMEM((ITERS + 1, CHIPS, 1, TILE), F32),
            pltpu.VMEM((ITERS, 16, 4096), BF16),
            pltpu.VMEM((ITERS, NX, 16, 512), BF16),
            pltpu.VMEM((ITERS, NX, 1, TILE), F32),
            pltpu.VMEM((16, TILE), F32),
            dma((groups,)), dma((groups,)), dma((groups,)), dma((2,)),
            dma, dma((ITERS, groups)), dma, dma((ITERS + 1,)),
            dma, dma((ITERS, groups)), dma, dma((ITERS,)), dma, dma((ITERS,)),
            dma((5,)), dma((5,)), dma((5,)),
        ],
        compiler_params=pltpu.CompilerParams(
            collective_id=0, has_side_effects=True, vmem_limit_bytes=40 * 2**20),
        name="cgls",
    )(activations, targets.T, counts, ridge[None, :])
    step = alpha[:, 0:1]
    return (w + step * p).T, (r - step * q).T


def solution(mesh):
    placed = (P("tok", "feat"), P("tok", None), P("tok"), P())
    return jax.shard_map(
        local,
        mesh=mesh,
        in_specs=placed,
        out_specs=(P("feat", None), P("tok", None)),
        check_vma=False,
    )
```

```python
import jax
import jax.numpy as jnp
from jax import lax
from jax.experimental import pallas as pl
from jax.experimental.pallas import tpu as pltpu
from jax.sharding import PartitionSpec as P

ITERS = 4
NY, NZ, NX = 4, 8, 4
CHIPS = NY * NZ
MESH = pl.DeviceIdType.MESH
F32, BF16 = jnp.float32, jnp.bfloat16


def hops(offset):
    dy, dz = offset
    return min(dy, NY - dy) + min(dz, NZ - dz)


OFFSETS = sorted(((dy, dz) for dy in range(NY) for dz in range(NZ)), key=lambda o: (-hops(o), o))
PEERS = CHIPS - 1
GROUPS = ((0, 1), (1, 5), (5, 12), (12, 20), (20, 27), (27, 32))
TILE = 128


def kernel(a_hbm, y_hbm, count_hbm, ridge_hbm, w_out, p_out, r_out, q_out, alpha_out,
           y_ref, count_ref, ridge_ref, in_sems, a, at, ysend, yrecv, mask, r, q, s, p, w, total, tsend, trecv, drow, ahead, g, xbuf, alpha_buf,
           load_sem, push_send, push_recv, y_sems, t_send, t_recv, d_send, d_recv,
           g_send, g_recv, x_send, x_recv, pub_local, pub_send, pub_recv):
    tok, x = lax.axis_index("tok"), lax.axis_index("feat")
    core = lax.rem(tok, 2)
    z, y = lax.rem(tok // 2, NZ), tok // (2 * NZ)
    chips = [lax.rem(y + dy, NY) * NZ + lax.rem(z + dz, NZ) for dy, dz in OFFSETS]
    me = chips[-1]
    mine = pl.ds(pl.multiple_of(core * 256, 256), 256)
    others = pl.ds(pl.multiple_of((1 - core) * 256, 256), 256)
    sibling = (me * 2 + 1 - core, x)
    peers = [(chip * 2 + core, x) for chip in chips[:PEERS]]
    x_peers = [(tok, lax.rem(x + d, NX)) for d in (2, 1, 3)]

    def tile(chip):
        return pl.ds(pl.multiple_of(chip * TILE, TILE), TILE)

    def slots(lo, hi):
        return slice(lo * TILE, hi * TILE)

    def send(src, dst, send_sem, recv_sem, device):
        copy = pltpu.make_async_remote_copy(
            src_ref=src, dst_ref=dst, send_sem=send_sem, recv_sem=recv_sem,
            device_id=device, device_id_type=MESH)
        copy.start()
        return copy

    def wait(ref, sem):
        pltpu.make_async_copy(ref, ref, sem).wait()

    barrier = pltpu.get_barrier_semaphore()
    for device in peers + x_peers + [sibling]:
        pl.semaphore_signal(barrier, inc=1, device_id=device, device_id_type=MESH)

    inputs = [
        pltpu.make_async_copy(src, dst, in_sems.at[k])
        for k, (src, dst) in enumerate(((count_hbm, count_ref), (y_hbm, y_ref), (ridge_hbm, ridge_ref)))]
    for copy in inputs:
        copy.start()
    for group, (lo, hi) in enumerate(GROUPS):
        for j in range(lo, hi):
            pltpu.make_async_copy(
                a_hbm.at[:, tile(chips[j])], a.at[mine, slots(j, j + 1)], load_sem.at[group]).start()

    for copy in inputs:
        copy.wait()
    live = (lax.broadcasted_iota(jnp.int32, (32, 256), 1) < count_ref[0]).astype(F32)
    own_rows = pl.ds(pl.multiple_of(core * 16, 16), 16)
    sibling_rows = pl.ds(pl.multiple_of((1 - core) * 16, 16), 16)
    ysend[0:16, :] = y_ref[sibling_rows, :] * live[0:16]
    ysend[16:24, :] = live[0:8]
    r[:, mine] = y_ref[own_rows, :] * live[0:16]
    mask[:, mine] = live[0:8]
    q[...] = jnp.zeros_like(q)
    p[...] = jnp.zeros_like(p)
    w[...] = jnp.zeros_like(w)
    total[...] = jnp.zeros_like(total)

    lane = lax.broadcasted_iota(jnp.int32, (16, TILE), 1)
    sub = lax.broadcasted_iota(jnp.int32, (16, TILE), 0)
    eye = (lane == sub).astype(F32)
    field = lane // 16
    pick = (lax.broadcasted_iota(jnp.int32, (16, 32), 1)
            == lax.broadcasted_iota(jnp.int32, (16, 32), 0) + core * 16).astype(F32)
    ridge = jnp.sum(ridge_ref[...] * pick, axis=1, keepdims=True)

    def to_row(column, which):
        return jnp.sum(column * which, axis=0, keepdims=True)

    def to_column(row, which):
        return jnp.sum(row * which, axis=1, keepdims=True)

    def lanes(v):
        out = v[:, 0:TILE]
        for j in range(1, v.shape[1] // TILE):
            out = out + v[:, j * TILE:(j + 1) * TILE]
        return jnp.sum(out, axis=1, keepdims=True)

    def pack(*columns):
        out = jnp.zeros((16, TILE), F32)
        for k, column in enumerate(columns):
            for place in range(3):
                head = column.astype(BF16).astype(F32)
                out = jnp.where(field == 3 * k + place, head, out)
                column = column - head
        return out.astype(BF16)

    def unpack(v):
        return [jnp.sum(jnp.where(field // 3 == k, v, 0.0), axis=1, keepdims=True) * 0.0625 for k in range(2)]

    def curvature(n):
        wait(drow.at[n, pl.ds(0, PEERS)], d_recv.at[n])
        row = drow[n, 0]
        for j in range(1, CHIPS):
            row = row + drow[n, j]
        return to_column(row, eye)

    def send_row(n, j):
        send(drow.at[n, me], drow.at[n, me], d_send, d_recv.at[n], peers[j])

    pl.semaphore_wait(barrier, PEERS + NX)

    y_copy = send(ysend, yrecv, y_sems.at[0], y_sems.at[1], sibling)
    pushes = []
    for group, (lo, hi) in enumerate(GROUPS):
        wait(a.at[mine, slots(lo, hi)], load_sem.at[group])
        part = a.at[mine, slots(lo, hi)]
        pushes.append(send(part, part, push_send.at[group], push_recv.at[group], sibling))
    y_copy.wait()
    r[:, others] = yrecv[0:16, :]
    mask[:, others] = yrecv[16:24, :]
    s[...] = r[...].astype(BF16)
    drow[0, me] = to_row(lanes(r[...] * r[...]), eye)

    def step(n, carry):
        gamma, norm, guess, beta = carry
        first = n == 0
        inv_gamma, inv_guess = 1.0 / gamma, 1.0 / guess
        for group, (lo, hi) in enumerate(GROUPS):
            @pl.when(n == 0)
            def _():
                pushes[group].wait_recv()
            part = jnp.dot(s[...], a[:, slots(lo, hi)], preferred_element_type=F32)
            tsend[n, :, slots(lo, hi)] = part.astype(BF16)
            for j in range(lo, min(hi, PEERS)):
                send(tsend.at[n, :, slots(j, j + 1)], trecv.at[n, j], t_send, t_recv.at[n, group], peers[j])
            if hi == CHIPS:
                summed = part[:, (PEERS - lo) * TILE:]
        for j in range(PEERS):
            send_row(n, j)

        @pl.when(n == 0)
        def _():
            for lo, hi in GROUPS:
                at[slots(lo, hi), :] = a[:, slots(lo, hi)].T

        @pl.when(n > 0)
        def _():
            p[...] = g[...].astype(F32) + beta * p[...]

        summed = summed - ridge * (w[:, tile(me)] + guess * p[:, tile(me)])
        for group, (lo, hi) in reversed(list(enumerate(GROUPS))):
            hi = min(hi, PEERS)
            wait(trecv.at[n, pl.ds(lo, hi - lo)], t_recv.at[n, group])
            for j in range(lo, hi):
                summed = summed + trecv[n, j].astype(F32)
        ahead[n, :, tile(me)] = summed.astype(BF16)
        for group, (lo, hi) in enumerate(GROUPS):
            for j in range(lo, min(hi, PEERS)):
                part = ahead.at[n, :, tile(me)]
                send(part, part, g_send, g_recv.at[n, group], peers[j])

        energy = curvature(n)
        alpha = jnp.where(first, 0.0, gamma / (energy + ridge * norm))
        ratio = jnp.where(first, 1.0, alpha * inv_guess)
        r[...] = r[...] - alpha * q[...]
        w[...] = w[...] + alpha * p[...]
        total[...] = (1.0 - ratio) * total[...]

        image = jnp.zeros((16, 512), F32)
        for group, (lo, hi) in reversed(list(enumerate(GROUPS))):
            wait(ahead.at[n, :, slots(0, min(hi, PEERS) - lo)], g_recv.at[n, group])
            for j in reversed(range(lo, hi)):
                at_j = tile(chips[j])
                grad = total[:, at_j] + ratio * ahead[n, :, at_j].astype(F32)
                total[:, at_j] = grad
                grad = grad.astype(BF16)
                g[:, at_j] = grad
                image = image + jnp.dot(grad, at[slots(j, j + 1), :], preferred_element_type=F32)
        grad = g[...].astype(F32)
        xbuf[n, x, :, 512:] = pack(lanes(grad * grad), lanes(grad * p[...]))
        xbuf[n, x, :, 0:512] = image.astype(BF16)
        for device in x_peers:
            send(xbuf.at[n, x], xbuf.at[n, x], x_send, x_recv.at[n], device)
        wait(xbuf.at[n, pl.ds(0, NX - 1)], x_recv.at[n])
        image = ((xbuf[n, 0].astype(F32) + xbuf[n, 1].astype(F32))
                 + (xbuf[n, 2].astype(F32) + xbuf[n, 3].astype(F32)))
        gamma_new, cross = unpack(image[:, 512:])
        beta = jnp.where(first, 0.0, gamma_new * inv_gamma)
        norm = gamma_new + 2.0 * beta * cross + beta * beta * norm
        guess = jnp.where(first, (2.0 / 3.0) * energy / gamma_new, 1.15 * alpha)
        fresh_q = image[:, 0:512] * mask[0:1, :] + beta * q[...]
        q[...] = fresh_q
        s[...] = (r[...] - guess * fresh_q).astype(BF16)
        drow[n + 1, me] = to_row(lanes(fresh_q * fresh_q), eye)
        return gamma_new, norm, guess, beta

    one = jnp.ones((16, 1), F32)
    gamma, norm, guess, beta = lax.fori_loop(0, ITERS, step, (one, one, one, one))

    for j in range(PEERS):
        send_row(ITERS, j)

    def publish(k, here, there, out):
        pltpu.make_async_copy(here, out.at[own_rows], pub_local.at[k]).start()
        send(there, out.at[own_rows], pub_send.at[k], pub_recv.at[k], sibling)

    publish(0, w, w, w_out)
    publish(1, r.at[:, mine], r.at[:, others], r_out)
    publish(2, q.at[:, mine], q.at[:, others], q_out)
    p[...] = g[...].astype(F32) + beta * p[...]
    publish(3, p, p, p_out)
    alpha = gamma / (curvature(ITERS) + ridge * norm)
    alpha_buf[...] = jnp.broadcast_to(alpha, alpha_buf.shape)
    publish(4, alpha_buf, alpha_buf, alpha_out)
    for k, (src, out) in enumerate(((w, w_out), (r.at[:, mine], r_out), (q.at[:, mine], q_out),
                                    (p, p_out), (alpha_buf, alpha_out))):
        wait(src, pub_local.at[k])
        wait(src, pub_send.at[k])
        wait(out.at[sibling_rows], pub_recv.at[k])
    for push in pushes:
        push.wait_send()
    wait(tsend.at[:, :, slots(0, PEERS)], t_send)
    wait(ahead.at[:, :, slots(0, PEERS)], g_send)
    wait(drow.at[:, pl.ds(0, PEERS)], d_send)
    wait(xbuf.at[:, pl.ds(0, NX - 1)], x_send)


PARTS = 4


def finish(w_hbm, p_hbm, r_hbm, q_hbm, alpha_hbm, w_out, r_out, w, p, r, q, alpha, in_sems, out_sems):
    width = w.shape[1] // PARTS
    parts = [(slice(None), slice(k * width, (k + 1) * width)) for k in range(PARTS)]
    small = [
        pltpu.make_async_copy(src, dst, in_sems.at[k])
        for k, (src, dst) in enumerate(((alpha_hbm, alpha), (r_hbm, r), (q_hbm, q)))]
    large = [
        pltpu.make_async_copy(src.at[part], dst.at[part], in_sems.at[3 + 2 * k + which])
        for k, part in enumerate(parts) for which, (src, dst) in enumerate(((w_hbm, w), (p_hbm, p)))]
    for copy in small + large:
        copy.start()
    for copy in small:
        copy.wait()
    step = alpha[:, 0:1]
    r[...] = r[...] - step * q[...]
    stores = [pltpu.make_async_copy(r, r_out, out_sems.at[PARTS])]
    stores[0].start()
    for k, part in enumerate(parts):
        large[2 * k].wait()
        large[2 * k + 1].wait()
        w[part] = w[part] + step * p[part]
        store = pltpu.make_async_copy(w.at[part], w_out.at[part], out_sems.at[k])
        store.start()
        stores.append(store)
    for store in stores:
        store.wait()


def local(activations, targets, counts, ridge):
    any_ = pl.BlockSpec(memory_space=pl.ANY)
    hbm = pl.BlockSpec(memory_space=pltpu.HBM)
    dma = pltpu.SemaphoreType.DMA
    groups = len(GROUPS)
    w, p, r, q, alpha = pl.pallas_call(
        kernel,
        out_shape=[jax.ShapeDtypeStruct((32, n), F32) for n in (4096, 4096, 256, 256, TILE)],
        in_specs=[hbm] * 4,
        out_specs=[any_] * 5,
        scratch_shapes=[
            pltpu.VMEM((32, 256), F32),
            pltpu.SMEM((1,), jnp.int32),
            pltpu.VMEM((1, 32), F32),
            dma((3,)),
            pltpu.VMEM((512, 4096), BF16),
            pltpu.VMEM((4096, 512), BF16),
            pltpu.VMEM((24, 256), F32),
            pltpu.VMEM((24, 256), F32),
            pltpu.VMEM((8, 512), F32),
            pltpu.VMEM((16, 512), F32),
            pltpu.VMEM((16, 512), F32),
            pltpu.VMEM((16, 512), BF16),
            pltpu.VMEM((16, 4096), F32),
            pltpu.VMEM((16, 4096), F32),
            pltpu.VMEM((16, 4096), F32),
            pltpu.VMEM((ITERS, 16, 4096), BF16),
            pltpu.VMEM((ITERS, PEERS, 16, TILE), BF16),
            pltpu.VMEM((ITERS + 1, CHIPS, 1, TILE), F32),
            pltpu.VMEM((ITERS, 16, 4096), BF16),
            pltpu.VMEM((16, 4096), BF16),
            pltpu.VMEM((ITERS, NX, 16, 512 + TILE), BF16),
            pltpu.VMEM((16, TILE), F32),
            dma((groups,)), dma((groups,)), dma((groups,)), dma((2,)),
            dma, dma((ITERS, groups)), dma, dma((ITERS + 1,)),
            dma, dma((ITERS, groups)), dma, dma((ITERS,)),
            dma((5,)), dma((5,)), dma((5,)),
        ],
        compiler_params=pltpu.CompilerParams(
            collective_id=0, has_side_effects=True, vmem_limit_bytes=58 * 2**20),
        name="cgls",
    )(activations, targets.T, counts, ridge[None, :])
    w, r = pl.pallas_call(
        finish,
        out_shape=[jax.ShapeDtypeStruct((32, n), F32) for n in (4096, 256)],
        in_specs=[hbm] * 5,
        out_specs=[any_] * 2,
        scratch_shapes=[
            pltpu.VMEM((32, 4096), F32), pltpu.VMEM((32, 4096), F32),
            pltpu.VMEM((32, 256), F32), pltpu.VMEM((32, 256), F32), pltpu.VMEM((32, TILE), F32),
            dma((2 * PARTS + 3,)), dma((PARTS + 1,)),
        ],
        compiler_params=pltpu.CompilerParams(vmem_limit_bytes=58 * 2**20),
        name="finish",
    )(w, p, r, q, alpha)
    return w.T, r.T


def solution(mesh):
    placed = (P("tok", "feat"), P("tok", None), P("tok"), P())
    return jax.shard_map(
        local,
        mesh=mesh,
        in_specs=placed,
        out_specs=(P("feat", None), P("tok", None)),
        check_vma=False,
    )
```

```python
import jax
import jax.numpy as jnp
from jax import lax
from jax.experimental import pallas as pl
from jax.experimental.pallas import tpu as pltpu
from jax.sharding import PartitionSpec as P

ITERS = 4
NY, NZ, NX = 4, 8, 4
CHIPS = NY * NZ
MESH = pl.DeviceIdType.MESH
F32, BF16 = jnp.float32, jnp.bfloat16


def hops(offset):
    dy, dz = offset
    return min(dy, NY - dy) + min(dz, NZ - dz)


OFFSETS = sorted(((dy, dz) for dy in range(NY) for dz in range(NZ)), key=lambda o: (-hops(o), o))
PEERS = CHIPS - 1
GROUPS = ((0, 1), (1, 5), (5, 12), (12, 20), (20, 27), (27, 32))
LATE = 2
TILE = 128


def kernel(a_hbm, y_hbm, count_hbm, ridge_hbm, w_out, r_out,
           y_ref, count_ref, ridge_ref, in_sems, a, at, ysend, yrecv, mask, r, q, s, p, w, total, tsend, trecv, drow, ahead, g, xbuf, dlast, state_out, state_in, w2, p2, r2, q2,
           load_sem, push_send, push_recv, y_sems, t_send, t_recv, d_send, d_recv,
           g_send, g_recv, x_send, x_recv, dl_send, dl_recv, pub_local, pub_send, pub_recv):
    tok, x = lax.axis_index("tok"), lax.axis_index("feat")
    core = lax.rem(tok, 2)
    z, y = lax.rem(tok // 2, NZ), tok // (2 * NZ)
    chips = [lax.rem(y + dy, NY) * NZ + lax.rem(z + dz, NZ) for dy, dz in OFFSETS]
    me = chips[-1]
    mine = pl.ds(pl.multiple_of(core * 256, 256), 256)
    others = pl.ds(pl.multiple_of((1 - core) * 256, 256), 256)
    sibling = (me * 2 + 1 - core, x)
    peers = [(chip * 2 + core, x) for chip in chips[:PEERS]]
    cross_peers = [(chip * 2 + 1 - core, x) for chip in chips[:PEERS]]
    x_peers = [(tok, lax.rem(x + d, NX)) for d in (2, 1, 3)]

    def tile(chip):
        return pl.ds(pl.multiple_of(chip * TILE, TILE), TILE)

    def slots(lo, hi):
        return slice(lo * TILE, hi * TILE)

    def send(src, dst, send_sem, recv_sem, device):
        copy = pltpu.make_async_remote_copy(
            src_ref=src, dst_ref=dst, send_sem=send_sem, recv_sem=recv_sem,
            device_id=device, device_id_type=MESH)
        copy.start()
        return copy

    def wait(ref, sem):
        pltpu.make_async_copy(ref, ref, sem).wait()

    barrier = pltpu.get_barrier_semaphore()
    for device in peers + x_peers + [sibling] + cross_peers:
        pl.semaphore_signal(barrier, inc=1, device_id=device, device_id_type=MESH)

    inputs = [
        pltpu.make_async_copy(src, dst, in_sems.at[k])
        for k, (src, dst) in enumerate(((count_hbm, count_ref), (y_hbm, y_ref), (ridge_hbm, ridge_ref)))]
    for copy in inputs:
        copy.start()
    for group, (lo, hi) in enumerate(GROUPS):
        for j in range(lo, hi):
            pltpu.make_async_copy(
                a_hbm.at[:, tile(chips[j])], a.at[mine, slots(j, j + 1)], load_sem.at[group]).start()

    for copy in inputs:
        copy.wait()
    live = (lax.broadcasted_iota(jnp.int32, (32, 256), 1) < count_ref[0]).astype(F32)
    own_rows = pl.ds(pl.multiple_of(core * 16, 16), 16)
    sibling_rows = pl.ds(pl.multiple_of((1 - core) * 16, 16), 16)
    ysend[0:16, :] = y_ref[sibling_rows, :] * live[0:16]
    ysend[16:24, :] = live[0:8]
    r[:, mine] = y_ref[own_rows, :] * live[0:16]
    mask[:, mine] = live[0:8]
    q[...] = jnp.zeros_like(q)
    p[...] = jnp.zeros_like(p)
    w[...] = jnp.zeros_like(w)
    total[...] = jnp.zeros_like(total)

    lane = lax.broadcasted_iota(jnp.int32, (16, TILE), 1)
    sub = lax.broadcasted_iota(jnp.int32, (16, TILE), 0)
    eye = (lane == sub).astype(F32)
    field = lane // 16
    def ridge_of(which):
        pick = (lax.broadcasted_iota(jnp.int32, (16, 32), 1)
                == lax.broadcasted_iota(jnp.int32, (16, 32), 0) + which * 16).astype(F32)
        return jnp.sum(ridge_ref[...] * pick, axis=1, keepdims=True)

    ridge, ridge2 = ridge_of(core), ridge_of(1 - core)

    def to_row(column, which):
        return jnp.sum(column * which, axis=0, keepdims=True)

    def to_column(row, which):
        return jnp.sum(row * which, axis=1, keepdims=True)

    def lanes(v):
        out = v[:, 0:TILE]
        for j in range(1, v.shape[1] // TILE):
            out = out + v[:, j * TILE:(j + 1) * TILE]
        return jnp.sum(out, axis=1, keepdims=True)

    def pack(*columns):
        out = jnp.zeros((16, TILE), F32)
        for k, column in enumerate(columns):
            for place in range(3):
                head = column.astype(BF16).astype(F32)
                out = jnp.where(field == 3 * k + place, head, out)
                column = column - head
        return out.astype(BF16)

    def unpack(v):
        return [jnp.sum(jnp.where(field // 3 == k, v, 0.0), axis=1, keepdims=True) * 0.0625 for k in range(2)]

    def curvature(n):
        wait(drow.at[n, pl.ds(0, PEERS)], d_recv.at[n])
        row = drow[n, 0]
        for j in range(1, CHIPS):
            row = row + drow[n, j]
        return to_column(row, eye)

    def last_curvature(which):
        row = dlast[which * CHIPS]
        for j in range(1, CHIPS):
            row = row + dlast[which * CHIPS + j]
        return to_column(row, eye)

    def send_row(n, j):
        send(drow.at[n, me], drow.at[n, me], d_send, d_recv.at[n], peers[j])

    pl.semaphore_wait(barrier, 2 * PEERS + NX)

    y_copy = send(ysend, yrecv, y_sems.at[0], y_sems.at[1], sibling)
    pushes = []
    for group, (lo, hi) in enumerate(GROUPS):
        wait(a.at[mine, slots(lo, hi)], load_sem.at[group])
        part = a.at[mine, slots(lo, hi)]
        pushes.append(send(part, part, push_send.at[group], push_recv.at[group], sibling))
    y_copy.wait()
    r[:, others] = yrecv[0:16, :]
    mask[:, others] = yrecv[16:24, :]
    s[...] = r[...].astype(BF16)
    drow[0, me] = to_row(lanes(r[...] * r[...]), eye)

    def step(n, carry):
        gamma, norm, guess, beta = carry
        first = n == 0
        inv_gamma, inv_guess = 1.0 / gamma, 1.0 / guess
        for group, (lo, hi) in enumerate(GROUPS):
            @pl.when(n == 0)
            def _():
                pushes[group].wait_recv()
            part = jnp.dot(s[...], a[:, slots(lo, hi)], preferred_element_type=F32)
            tsend[n, :, slots(lo, hi)] = part.astype(BF16)
            for j in range(lo, min(hi, PEERS)):
                send(tsend.at[n, :, slots(j, j + 1)], trecv.at[n, j], t_send, t_recv.at[n, group], peers[j])
            if hi == CHIPS:
                summed = part[:, (PEERS - lo) * TILE:]
        for j in range(PEERS):
            send_row(n, j)

        @pl.when(n == 0)
        def _():
            for lo, hi in GROUPS:
                at[slots(lo, hi), :] = a[:, slots(lo, hi)].T

        @pl.when(n > 0)
        def _():
            p[...] = g[...].astype(F32) + beta * p[...]

        summed = summed - ridge * (w[:, tile(me)] + guess * p[:, tile(me)])
        for group, (lo, hi) in reversed(list(enumerate(GROUPS))):
            hi = min(hi, PEERS)
            wait(trecv.at[n, pl.ds(lo, hi - lo)], t_recv.at[n, group])
            for j in range(lo, hi):
                summed = summed + trecv[n, j].astype(F32)
        ahead[n, :, tile(me)] = summed.astype(BF16)
        for group, (lo, hi) in enumerate(GROUPS):
            for j in range(lo, min(hi, PEERS)):
                part = ahead.at[n, :, tile(me)]
                send(part, part, g_send, g_recv.at[n, group], peers[j])

        energy = curvature(n)
        alpha = jnp.where(first, 0.0, gamma / (energy + ridge * norm))
        ratio = jnp.where(first, 1.0, alpha * inv_guess)
        r[...] = r[...] - alpha * q[...]
        w[...] = w[...] + alpha * p[...]
        total[...] = (1.0 - ratio) * total[...]

        image = jnp.zeros((16, 512), F32)
        for last in (LATE, *range(LATE + 1, len(GROUPS)))[::-1]:
            for group in range(LATE, -1, -1) if last == LATE else (last,):
                lo, hi = GROUPS[group]
                wait(ahead.at[n, :, slots(0, min(hi, PEERS) - lo)], g_recv.at[n, group])
            for j in reversed(range(0 if last == LATE else lo, GROUPS[last][1])):
                at_j = tile(chips[j])
                grad = total[:, at_j] + ratio * ahead[n, :, at_j].astype(F32)
                total[:, at_j] = grad
                grad = grad.astype(BF16)
                g[:, at_j] = grad
                image = image + jnp.dot(grad, at[slots(j, j + 1), :], preferred_element_type=F32)
        grad = g[...].astype(F32)
        xbuf[n, x, :, 512:] = pack(lanes(grad * grad), lanes(grad * p[...]))
        xbuf[n, x, :, 0:512] = image.astype(BF16)
        for device in x_peers:
            send(xbuf.at[n, x], xbuf.at[n, x], x_send, x_recv.at[n], device)
        wait(xbuf.at[n, pl.ds(0, NX - 1)], x_recv.at[n])
        image = ((xbuf[n, 0].astype(F32) + xbuf[n, 1].astype(F32))
                 + (xbuf[n, 2].astype(F32) + xbuf[n, 3].astype(F32)))
        gamma_new, cross = unpack(image[:, 512:])
        beta = jnp.where(first, 0.0, gamma_new * inv_gamma)
        norm = gamma_new + 2.0 * beta * cross + beta * beta * norm
        guess = jnp.where(first, (2.0 / 3.0) * energy / gamma_new, 1.15 * alpha)
        fresh_q = image[:, 0:512] * mask[0:1, :] + beta * q[...]
        q[...] = fresh_q
        s[...] = (r[...] - guess * fresh_q).astype(BF16)
        drow[n + 1, me] = to_row(lanes(fresh_q * fresh_q), eye)
        return gamma_new, norm, guess, beta

    one = jnp.ones((16, 1), F32)
    gamma, norm, guess, beta = lax.fori_loop(0, ITERS, step, (one, one, one, one))

    for j in range(PEERS):
        for device in (peers[j], cross_peers[j]):
            send(drow.at[ITERS, me], dlast.at[core * CHIPS + me], dl_send, dl_recv, device)
    send(drow.at[ITERS, me], dlast.at[core * CHIPS + me], dl_send, dl_recv, sibling)
    dlast[core * CHIPS + me] = drow[ITERS, me]
    state_out[0] = jnp.broadcast_to(gamma, (16, TILE))
    state_out[1] = jnp.broadcast_to(norm, (16, TILE))
    send(state_out, state_in, pub_send.at[0], pub_recv.at[0], sibling)
    send(w, w2, pub_send.at[1], pub_recv.at[1], sibling)
    send(r.at[:, others], r2, pub_send.at[2], pub_recv.at[2], sibling)
    send(q.at[:, others], q2, pub_send.at[3], pub_recv.at[3], sibling)
    p[...] = g[...].astype(F32) + beta * p[...]
    send(p, p2, pub_send.at[4], pub_recv.at[4], sibling)
    for k, ref in enumerate((state_in, w2, r2, q2, p2)):
        wait(ref, pub_recv.at[k])
        wait(ref, pub_send.at[k])
    wait(dlast.at[pl.ds(0, 2 * CHIPS - 1)], dl_recv)
    alpha = gamma / (last_curvature(core) + ridge * norm)
    alpha2 = state_in[0, :, 0:1] / (last_curvature(1 - core) + ridge2 * state_in[1, :, 0:1])
    w[...] = w[...] + alpha * p[...]
    w2[...] = w2[...] + alpha2 * p2[...]
    r[:, mine] = r[:, mine] - alpha * q[:, mine]
    r2[...] = r2[...] - alpha2 * q2[...]
    outs = [pltpu.make_async_copy(src, dst, pub_local.at[k]) for k, (src, dst) in enumerate((
        (w, w_out.at[own_rows]), (w2, w_out.at[sibling_rows]),
        (r.at[:, mine], r_out.at[own_rows]), (r2, r_out.at[sibling_rows])))]
    for copy in outs:
        copy.start()
    for copy in outs:
        copy.wait()
    for push in pushes:
        push.wait_send()
    wait(tsend.at[:, :, slots(0, PEERS)], t_send)
    wait(ahead.at[:, :, slots(0, PEERS)], g_send)
    wait(drow.at[pl.ds(0, ITERS), pl.ds(0, PEERS)], d_send)
    wait(dlast.at[pl.ds(0, 2 * CHIPS - 1)], dl_send)
    wait(xbuf.at[:, pl.ds(0, NX - 1)], x_send)


def hand_over(w_in, r_in, w_out, r_out, w, r, sems):
    parts = [(r_in, r, r_out)] + [
        (w_in.at[rows], w.at[rows], w_out.at[rows]) for rows in (pl.ds(8 * k, 8) for k in range(4))]
    loads = [pltpu.make_async_copy(src, at, sems.at[0, k]) for k, (src, at, _) in enumerate(parts)]
    stores = [pltpu.make_async_copy(at, dst, sems.at[1, k]) for k, (_, at, dst) in enumerate(parts)]
    for load in loads:
        load.start()
    for load, store in zip(loads, stores):
        load.wait()
        store.start()
    for store in stores:
        store.wait()


def local(activations, targets, counts, ridge):
    any_ = pl.BlockSpec(memory_space=pl.ANY)
    hbm = pl.BlockSpec(memory_space=pltpu.HBM)
    dma = pltpu.SemaphoreType.DMA
    groups = len(GROUPS)
    w, r = pl.pallas_call(
        kernel,
        out_shape=[jax.ShapeDtypeStruct((32, n), F32) for n in (4096, 256)],
        in_specs=[hbm] * 4,
        out_specs=[any_] * 2,
        scratch_shapes=[
            pltpu.VMEM((32, 256), F32),
            pltpu.SMEM((1,), jnp.int32),
            pltpu.VMEM((1, 32), F32),
            dma((3,)),
            pltpu.VMEM((512, 4096), BF16),
            pltpu.VMEM((4096, 512), BF16),
            pltpu.VMEM((24, 256), F32),
            pltpu.VMEM((24, 256), F32),
            pltpu.VMEM((8, 512), F32),
            pltpu.VMEM((16, 512), F32),
            pltpu.VMEM((16, 512), F32),
            pltpu.VMEM((16, 512), BF16),
            pltpu.VMEM((16, 4096), F32),
            pltpu.VMEM((16, 4096), F32),
            pltpu.VMEM((16, 4096), F32),
            pltpu.VMEM((ITERS, 16, 4096), BF16),
            pltpu.VMEM((ITERS, PEERS, 16, TILE), BF16),
            pltpu.VMEM((ITERS + 1, CHIPS, 1, TILE), F32),
            pltpu.VMEM((ITERS, 16, 4096), BF16),
            pltpu.VMEM((16, 4096), BF16),
            pltpu.VMEM((ITERS, NX, 16, 512 + TILE), BF16),
            pltpu.VMEM((2 * CHIPS, 1, TILE), F32),
            pltpu.VMEM((2, 16, TILE), F32),
            pltpu.VMEM((2, 16, TILE), F32),
            pltpu.VMEM((16, 4096), F32),
            pltpu.VMEM((16, 4096), F32),
            pltpu.VMEM((16, 256), F32),
            pltpu.VMEM((16, 256), F32),
            dma((groups,)), dma((groups,)), dma((groups,)), dma((2,)),
            dma, dma((ITERS, groups)), dma, dma((ITERS + 1,)),
            dma, dma((ITERS, groups)), dma, dma((ITERS,)), dma, dma,
            dma((5,)), dma((5,)), dma((5,)),
        ],
        compiler_params=pltpu.CompilerParams(
            collective_id=0, has_side_effects=True, vmem_limit_bytes=58 * 2**20),
        name="cgls",
    )(activations, targets.T, counts, ridge[None, :])
    w, r = pl.pallas_call(
        hand_over,
        out_shape=[jax.ShapeDtypeStruct((32, n), F32) for n in (4096, 256)],
        in_specs=[hbm] * 2,
        out_specs=[any_] * 2,
        scratch_shapes=[pltpu.VMEM((32, 4096), F32), pltpu.VMEM((32, 256), F32), dma((2, 5))],
        compiler_params=pltpu.CompilerParams(vmem_limit_bytes=58 * 2**20),
        name="hand_over",
    )(w, r)
    return w.T, r.T


def solution(mesh):
    placed = (P("tok", "feat"), P("tok", None), P("tok"), P())
    return jax.shard_map(
        local,
        mesh=mesh,
        in_specs=placed,
        out_specs=(P("feat", None), P("tok", None)),
        check_vma=False,
    )
```

```python
import jax
import jax.numpy as jnp
from jax import lax
from jax.experimental import pallas as pl
from jax.experimental.pallas import tpu as pltpu
from jax.sharding import PartitionSpec as P

ITERS = 4
NY, NZ, NX = 4, 8, 4
CHIPS = NY * NZ
MESH = pl.DeviceIdType.MESH
F32, BF16 = jnp.float32, jnp.bfloat16


def hops(offset):
    dy, dz = offset
    return min(dy, NY - dy) + min(dz, NZ - dz)


OFFSETS = sorted(((dy, dz) for dy in range(NY) for dz in range(NZ)), key=lambda o: (-hops(o), o))
PEERS = CHIPS - 1
GROUPS = ((0, 1), (1, 5), (5, 12), (12, 20), (20, 27), (27, 32))
LATE = 2
FAR_GROUPS = 2
FAR = GROUPS[FAR_GROUPS - 1][1]
TILE = 128


def kernel(a_hbm, y_hbm, count_hbm, ridge_hbm, w_out, r_out,
           y_ref, count_ref, ridge_ref, in_sems, a, at, ysend, yrecv, mask, r, q, s, p, w, total, tsend, trecv, fsend, fextra, drow, ahead, g, xbuf, dlast, state_out, state_in, w2, p2, r2, q2,
           load_sem, push_send, push_recv, y_sems, t_send, t_recv, f_send, f_recv, d_send, d_recv,
           g_send, g_recv, x_send, x_recv, dl_send, dl_recv, pub_local, pub_send, pub_recv):
    tok, x = lax.axis_index("tok"), lax.axis_index("feat")
    core = lax.rem(tok, 2)
    z, y = lax.rem(tok // 2, NZ), tok // (2 * NZ)
    chips = [lax.rem(y + dy, NY) * NZ + lax.rem(z + dz, NZ) for dy, dz in OFFSETS]
    me = chips[-1]
    mine = pl.ds(pl.multiple_of(core * 256, 256), 256)
    others = pl.ds(pl.multiple_of((1 - core) * 256, 256), 256)
    sibling = (me * 2 + 1 - core, x)
    peers = [(chip * 2 + core, x) for chip in chips[:PEERS]]
    cross_peers = [(chip * 2 + 1 - core, x) for chip in chips[:PEERS]]
    x_peers = [(tok, lax.rem(x + d, NX)) for d in (2, 1, 3)]

    def tile(chip):
        return pl.ds(pl.multiple_of(chip * TILE, TILE), TILE)

    def slots(lo, hi):
        return slice(lo * TILE, hi * TILE)

    def send(src, dst, send_sem, recv_sem, device):
        copy = pltpu.make_async_remote_copy(
            src_ref=src, dst_ref=dst, send_sem=send_sem, recv_sem=recv_sem,
            device_id=device, device_id_type=MESH)
        copy.start()
        return copy

    def wait(ref, sem):
        pltpu.make_async_copy(ref, ref, sem).wait()

    barrier = pltpu.get_barrier_semaphore()
    for device in peers + x_peers + [sibling] + cross_peers:
        pl.semaphore_signal(barrier, inc=1, device_id=device, device_id_type=MESH)

    inputs = [
        pltpu.make_async_copy(src, dst, in_sems.at[k])
        for k, (src, dst) in enumerate(((count_hbm, count_ref), (y_hbm, y_ref), (ridge_hbm, ridge_ref)))]
    for copy in inputs:
        copy.start()
    for group, (lo, hi) in enumerate(GROUPS):
        for j in range(lo, hi):
            pltpu.make_async_copy(
                a_hbm.at[:, tile(chips[j])], a.at[mine, slots(j, j + 1)], load_sem.at[group]).start()

    for copy in inputs:
        copy.wait()
    live = (lax.broadcasted_iota(jnp.int32, (32, 256), 1) < count_ref[0]).astype(F32)
    own_rows = pl.ds(pl.multiple_of(core * 16, 16), 16)
    sibling_rows = pl.ds(pl.multiple_of((1 - core) * 16, 16), 16)
    ysend[0:16, :] = y_ref[sibling_rows, :] * live[0:16]
    ysend[16:24, :] = live[0:8]
    r[:, mine] = y_ref[own_rows, :] * live[0:16]
    mask[:, mine] = live[0:8]
    q[...] = jnp.zeros_like(q)
    p[...] = jnp.zeros_like(p)
    w[...] = jnp.zeros_like(w)
    total[...] = jnp.zeros_like(total)

    lane = lax.broadcasted_iota(jnp.int32, (16, TILE), 1)
    sub = lax.broadcasted_iota(jnp.int32, (16, TILE), 0)
    eye = (lane == sub).astype(F32)
    field = lane // 16
    def ridge_of(which):
        pick = (lax.broadcasted_iota(jnp.int32, (16, 32), 1)
                == lax.broadcasted_iota(jnp.int32, (16, 32), 0) + which * 16).astype(F32)
        return jnp.sum(ridge_ref[...] * pick, axis=1, keepdims=True)

    ridge, ridge2 = ridge_of(core), ridge_of(1 - core)

    def to_row(column, which):
        return jnp.sum(column * which, axis=0, keepdims=True)

    def to_column(row, which):
        return jnp.sum(row * which, axis=1, keepdims=True)

    def lanes(v):
        out = v[:, 0:TILE]
        for j in range(1, v.shape[1] // TILE):
            out = out + v[:, j * TILE:(j + 1) * TILE]
        return jnp.sum(out, axis=1, keepdims=True)

    def pack(*columns):
        out = jnp.zeros((16, TILE), F32)
        for k, column in enumerate(columns):
            for place in range(3):
                head = column.astype(BF16).astype(F32)
                out = jnp.where(field == 3 * k + place, head, out)
                column = column - head
        return out.astype(BF16)

    def unpack(v):
        return [jnp.sum(jnp.where(field // 3 == k, v, 0.0), axis=1, keepdims=True) * 0.0625 for k in range(2)]

    def curvature(n):
        wait(drow.at[n, pl.ds(0, PEERS)], d_recv.at[n])
        row = drow[n, 0]
        for j in range(1, CHIPS):
            row = row + drow[n, j]
        return to_column(row, eye)

    def last_curvature(which):
        row = dlast[which * CHIPS]
        for j in range(1, CHIPS):
            row = row + dlast[which * CHIPS + j]
        return to_column(row, eye)

    def send_row(n, j):
        send(drow.at[n, me], drow.at[n, me], d_send, d_recv.at[n], peers[j])

    for group in range(FAR_GROUPS):
        wait(a.at[mine, slots(*GROUPS[group])], load_sem.at[group])
    for k, rows in enumerate((r[:, mine], ysend[0:16, :])):
        fsend[k] = jnp.dot(rows.astype(BF16), a[mine, slots(0, FAR)], preferred_element_type=F32).astype(BF16)

    pl.semaphore_wait(barrier, 2 * PEERS + NX)

    for group in range(FAR_GROUPS):
        for j in range(*GROUPS[group]):
            send(fsend.at[0, :, slots(j, j + 1)], trecv.at[0, j], t_send, t_recv.at[0, group], peers[j])
            send(fsend.at[1, :, slots(j, j + 1)], fextra.at[j], f_send, f_recv, cross_peers[j])

    y_copy = send(ysend, yrecv, y_sems.at[0], y_sems.at[1], sibling)
    pushes = {}
    for group in (*range(FAR_GROUPS, len(GROUPS)), *range(FAR_GROUPS)):
        part = a.at[mine, slots(*GROUPS[group])]
        if group >= FAR_GROUPS:
            wait(part, load_sem.at[group])
        pushes[group] = send(part, part, push_send.at[group], push_recv.at[group], sibling)
    y_copy.wait()
    r[:, others] = yrecv[0:16, :]
    mask[:, others] = yrecv[16:24, :]
    s[...] = r[...].astype(BF16)

    def step(n, carry):
        gamma, norm, guess, beta = carry
        first = n == 0
        inv_gamma, inv_guess = 1.0 / gamma, 1.0 / guess
        def scatter(group, lo, hi):
            part = jnp.dot(s[...], a[:, slots(lo, hi)], preferred_element_type=F32)
            tsend[n, :, slots(lo, hi)] = part.astype(BF16)
            for j in range(lo, min(hi, PEERS)):
                send(tsend.at[n, :, slots(j, j + 1)], trecv.at[n, j], t_send, t_recv.at[n, group], peers[j])
            return part

        for group, (lo, hi) in enumerate(GROUPS):
            if group < FAR_GROUPS:
                @pl.when(n > 0)
                def _():
                    scatter(group, lo, hi)
                continue

            @pl.when(n == 0)
            def _():
                pushes[group].wait_recv()
            part = scatter(group, lo, hi)
            if hi == CHIPS:
                summed = part[:, (PEERS - lo) * TILE:]
        rows = jnp.where(first, r[...], q[...])
        drow[n, me] = to_row(lanes(rows * rows), eye)
        for j in range(PEERS):
            send_row(n, j)

        @pl.when(n == 0)
        def _():
            for group in range(FAR_GROUPS):
                pushes[group].wait_recv()
            for lo, hi in GROUPS:
                at[slots(lo, hi), :] = a[:, slots(lo, hi)].T

        @pl.when(n > 0)
        def _():
            p[...] = g[...].astype(F32) + beta * p[...]

        summed = summed - ridge * (w[:, tile(me)] + guess * p[:, tile(me)])
        for group, (lo, hi) in reversed(list(enumerate(GROUPS))):
            hi = min(hi, PEERS)
            wait(trecv.at[n, pl.ds(lo, hi - lo)], t_recv.at[n, group])
            for j in range(lo, hi):
                summed = summed + trecv[n, j].astype(F32)
        @pl.when(n == 0)
        def _():
            wait(fextra, f_recv)
        extra = fextra[0].astype(F32)
        for j in range(1, FAR):
            extra = extra + fextra[j].astype(F32)
        summed = summed + jnp.where(first, extra, 0.0)
        ahead[n, :, tile(me)] = summed.astype(BF16)
        for group, (lo, hi) in enumerate(GROUPS):
            for j in range(lo, min(hi, PEERS)):
                part = ahead.at[n, :, tile(me)]
                send(part, part, g_send, g_recv.at[n, group], peers[j])

        energy = curvature(n)
        alpha = jnp.where(first, 0.0, gamma / (energy + ridge * norm))
        ratio = jnp.where(first, 1.0, alpha * inv_guess)
        r[...] = r[...] - alpha * q[...]
        w[...] = w[...] + alpha * p[...]
        keep = 1.0 - ratio

        image = jnp.zeros((16, 512), F32)
        for last in (LATE, *range(LATE + 1, len(GROUPS)))[::-1]:
            for group in range(LATE, -1, -1) if last == LATE else (last,):
                lo, hi = GROUPS[group]
                wait(ahead.at[n, :, slots(0, min(hi, PEERS) - lo)], g_recv.at[n, group])
            for j in reversed(range(0 if last == LATE else lo, GROUPS[last][1])):
                at_j = tile(chips[j])
                grad = keep * total[:, at_j] + ratio * ahead[n, :, at_j].astype(F32)
                total[:, at_j] = grad
                grad = grad.astype(BF16)
                g[:, at_j] = grad
                image = image + jnp.dot(grad, at[slots(j, j + 1), :], preferred_element_type=F32)
        grad = g[...].astype(F32)
        xbuf[n, x, :, 512:] = pack(lanes(grad * grad), lanes(grad * p[...]))
        xbuf[n, x, :, 0:512] = image.astype(BF16)
        for device in x_peers:
            send(xbuf.at[n, x], xbuf.at[n, x], x_send, x_recv.at[n], device)
        wait(xbuf.at[n, pl.ds(0, NX - 1)], x_recv.at[n])
        image = ((xbuf[n, 0].astype(F32) + xbuf[n, 1].astype(F32))
                 + (xbuf[n, 2].astype(F32) + xbuf[n, 3].astype(F32)))
        gamma_new, cross = unpack(image[:, 512:])
        beta = jnp.where(first, 0.0, gamma_new * inv_gamma)
        norm = gamma_new + 2.0 * beta * cross + beta * beta * norm
        guess = jnp.where(first, (2.0 / 3.0) * energy / gamma_new, 1.15 * alpha)
        fresh_q = image[:, 0:512] * mask[0:1, :] + beta * q[...]
        q[...] = fresh_q
        s[...] = (r[...] - guess * fresh_q).astype(BF16)
        return gamma_new, norm, guess, beta

    one = jnp.ones((16, 1), F32)
    gamma, norm, guess, beta = lax.fori_loop(0, ITERS, step, (one, one, one, one))

    drow[ITERS, me] = to_row(lanes(q[...] * q[...]), eye)
    for j in range(PEERS):
        for device in (peers[j], cross_peers[j]):
            send(drow.at[ITERS, me], dlast.at[core * CHIPS + me], dl_send, dl_recv, device)
    send(drow.at[ITERS, me], dlast.at[core * CHIPS + me], dl_send, dl_recv, sibling)
    dlast[core * CHIPS + me] = drow[ITERS, me]
    state_out[0] = jnp.broadcast_to(gamma, (16, TILE))
    state_out[1] = jnp.broadcast_to(norm, (16, TILE))
    send(state_out, state_in, pub_send.at[0], pub_recv.at[0], sibling)
    send(w, w2, pub_send.at[1], pub_recv.at[1], sibling)
    send(r.at[:, others], r2, pub_send.at[2], pub_recv.at[2], sibling)
    send(q.at[:, others], q2, pub_send.at[3], pub_recv.at[3], sibling)
    p[...] = g[...].astype(F32) + beta * p[...]
    send(p, p2, pub_send.at[4], pub_recv.at[4], sibling)
    for k, ref in enumerate((state_in, w2, r2, q2, p2)):
        wait(ref, pub_recv.at[k])
        wait(ref, pub_send.at[k])
    wait(dlast.at[pl.ds(0, 2 * CHIPS - 1)], dl_recv)
    alpha = gamma / (last_curvature(core) + ridge * norm)
    alpha2 = state_in[0, :, 0:1] / (last_curvature(1 - core) + ridge2 * state_in[1, :, 0:1])
    w[...] = w[...] + alpha * p[...]
    w2[...] = w2[...] + alpha2 * p2[...]
    r[:, mine] = r[:, mine] - alpha * q[:, mine]
    r2[...] = r2[...] - alpha2 * q2[...]
    outs = [pltpu.make_async_copy(src, dst, pub_local.at[k]) for k, (src, dst) in enumerate((
        (w, w_out.at[own_rows]), (w2, w_out.at[sibling_rows]),
        (r.at[:, mine], r_out.at[own_rows]), (r2, r_out.at[sibling_rows])))]
    for copy in outs:
        copy.start()
    for copy in outs:
        copy.wait()
    for push in pushes.values():
        push.wait_send()
    wait(fextra, f_send)
    wait(tsend.at[:, :, slots(0, PEERS)], t_send)
    wait(ahead.at[:, :, slots(0, PEERS)], g_send)
    wait(drow.at[pl.ds(0, ITERS), pl.ds(0, PEERS)], d_send)
    wait(dlast.at[pl.ds(0, 2 * CHIPS - 1)], dl_send)
    wait(xbuf.at[:, pl.ds(0, NX - 1)], x_send)


def hand_over(w_in, r_in, w_out, r_out, w, r, sems):
    parts = [(r_in, r, r_out)] + [
        (w_in.at[rows], w.at[rows], w_out.at[rows]) for rows in (pl.ds(8 * k, 8) for k in range(4))]
    loads = [pltpu.make_async_copy(src, at, sems.at[0, k]) for k, (src, at, _) in enumerate(parts)]
    stores = [pltpu.make_async_copy(at, dst, sems.at[1, k]) for k, (_, at, dst) in enumerate(parts)]
    for load in loads:
        load.start()
    for load, store in zip(loads, stores):
        load.wait()
        store.start()
    for store in stores:
        store.wait()


def local(activations, targets, counts, ridge):
    any_ = pl.BlockSpec(memory_space=pl.ANY)
    hbm = pl.BlockSpec(memory_space=pltpu.HBM)
    dma = pltpu.SemaphoreType.DMA
    groups = len(GROUPS)
    w, r = pl.pallas_call(
        kernel,
        out_shape=[jax.ShapeDtypeStruct((32, n), F32) for n in (4096, 256)],
        in_specs=[hbm] * 4,
        out_specs=[any_] * 2,
        scratch_shapes=[
            pltpu.VMEM((32, 256), F32),
            pltpu.SMEM((1,), jnp.int32),
            pltpu.VMEM((1, 32), F32),
            dma((3,)),
            pltpu.VMEM((512, 4096), BF16),
            pltpu.VMEM((4096, 512), BF16),
            pltpu.VMEM((24, 256), F32),
            pltpu.VMEM((24, 256), F32),
            pltpu.VMEM((8, 512), F32),
            pltpu.VMEM((16, 512), F32),
            pltpu.VMEM((16, 512), F32),
            pltpu.VMEM((16, 512), BF16),
            pltpu.VMEM((16, 4096), F32),
            pltpu.VMEM((16, 4096), F32),
            pltpu.VMEM((16, 4096), F32),
            pltpu.VMEM((ITERS, 16, 4096), BF16),
            pltpu.VMEM((ITERS, PEERS, 16, TILE), BF16),
            pltpu.VMEM((2, 16, FAR * TILE), BF16),
            pltpu.VMEM((FAR, 16, TILE), BF16),
            pltpu.VMEM((ITERS + 1, CHIPS, 1, TILE), F32),
            pltpu.VMEM((ITERS, 16, 4096), BF16),
            pltpu.VMEM((16, 4096), BF16),
            pltpu.VMEM((ITERS, NX, 16, 512 + TILE), BF16),
            pltpu.VMEM((2 * CHIPS, 1, TILE), F32),
            pltpu.VMEM((2, 16, TILE), F32),
            pltpu.VMEM((2, 16, TILE), F32),
            pltpu.VMEM((16, 4096), F32),
            pltpu.VMEM((16, 4096), F32),
            pltpu.VMEM((16, 256), F32),
            pltpu.VMEM((16, 256), F32),
            dma((groups,)), dma((groups,)), dma((groups,)), dma((2,)),
            dma, dma((ITERS, groups)), dma, dma, dma, dma((ITERS + 1,)),
            dma, dma((ITERS, groups)), dma, dma((ITERS,)), dma, dma,
            dma((5,)), dma((5,)), dma((5,)),
        ],
        compiler_params=pltpu.CompilerParams(
            collective_id=0, has_side_effects=True, vmem_limit_bytes=58 * 2**20),
        name="cgls",
    )(activations, targets.T, counts, ridge[None, :])
    w, r = pl.pallas_call(
        hand_over,
        out_shape=[jax.ShapeDtypeStruct((32, n), F32) for n in (4096, 256)],
        in_specs=[hbm] * 2,
        out_specs=[any_] * 2,
        scratch_shapes=[pltpu.VMEM((32, 4096), F32), pltpu.VMEM((32, 256), F32), dma((2, 5))],
        compiler_params=pltpu.CompilerParams(vmem_limit_bytes=58 * 2**20),
        name="hand_over",
    )(w, r)
    return w.T, r.T


def solution(mesh):
    placed = (P("tok", "feat"), P("tok", None), P("tok"), P())
    return jax.shard_map(
        local,
        mesh=mesh,
        in_specs=placed,
        out_specs=(P("feat", None), P("tok", None)),
        check_vma=False,
    )
```

```python
import jax
import jax.numpy as jnp
from jax import lax
from jax.experimental import pallas as pl
from jax.experimental.pallas import tpu as pltpu
from jax.sharding import PartitionSpec as P

ITERS = 4
NY, NZ, NX = 4, 8, 4
CHIPS = NY * NZ
MESH = pl.DeviceIdType.MESH
F32, BF16 = jnp.float32, jnp.bfloat16


def hops(offset):
    dy, dz = offset
    return min(dy, NY - dy) + min(dz, NZ - dz)


OFFSETS = sorted(((dy, dz) for dy in range(NY) for dz in range(NZ)), key=lambda o: (-hops(o), min(o[1], NZ - o[1]), o))
PEERS = CHIPS - 1
GROUPS = ((0, 1), (1, 5), (5, 12), (12, 20), (20, 27), (27, 32))
LATE = 1
FAR_GROUPS = 2
FAR = GROUPS[FAR_GROUPS - 1][1]
TILE = 128


def add_up(parts):
    while len(parts) > 1:
        parts = [sum(parts[i + 1:i + 2], parts[i]) for i in range(0, len(parts), 2)]
    return parts[0]


def kernel(a_hbm, y_hbm, count_hbm, ridge_hbm, w_out, r_out,
           y_ref, count_ref, ridge_ref, in_sems, a, at, ysend, yrecv, mask, r, q, s, p, w, total, tsend, trecv, fsend, fextra, drow, ahead, g, xbuf, dlast, state_out, state_in, w2, p2, r2, q2,
           load_sem, push_send, push_recv, y_sems, t_send, t_recv, f_send, f_recv, d_send, d_recv,
           g_send, g_recv, x_send, x_recv, dl_send, dl_recv, pub_local, pub_send, pub_recv):
    tok, x = lax.axis_index("tok"), lax.axis_index("feat")
    core = lax.rem(tok, 2)
    z, y = lax.rem(tok // 2, NZ), tok // (2 * NZ)
    chips = [lax.rem(y + dy, NY) * NZ + lax.rem(z + dz, NZ) for dy, dz in OFFSETS]
    me = chips[-1]
    mine = pl.ds(pl.multiple_of(core * 256, 256), 256)
    others = pl.ds(pl.multiple_of((1 - core) * 256, 256), 256)
    sibling = (me * 2 + 1 - core, x)
    peers = [(chip * 2 + core, x) for chip in chips[:PEERS]]
    cross_peers = [(chip * 2 + 1 - core, x) for chip in chips[:PEERS]]
    x_peers = [(tok, lax.rem(x + d, NX)) for d in (2, 1, 3)]

    def tile(chip):
        return pl.ds(pl.multiple_of(chip * TILE, TILE), TILE)

    def slots(lo, hi):
        return slice(lo * TILE, hi * TILE)

    def send(src, dst, send_sem, recv_sem, device):
        copy = pltpu.make_async_remote_copy(
            src_ref=src, dst_ref=dst, send_sem=send_sem, recv_sem=recv_sem,
            device_id=device, device_id_type=MESH)
        copy.start()
        return copy

    def wait(ref, sem):
        pltpu.make_async_copy(ref, ref, sem).wait()

    barrier = pltpu.get_barrier_semaphore()
    for device in peers + x_peers + [sibling] + cross_peers:
        pl.semaphore_signal(barrier, inc=1, device_id=device, device_id_type=MESH)

    inputs = [
        pltpu.make_async_copy(src, dst, in_sems.at[k])
        for k, (src, dst) in enumerate(((count_hbm, count_ref), (y_hbm, y_ref), (ridge_hbm, ridge_ref)))]
    for copy in inputs:
        copy.start()
    for group, (lo, hi) in enumerate(GROUPS):
        for j in range(lo, hi):
            pltpu.make_async_copy(
                a_hbm.at[:, tile(chips[j])], a.at[mine, slots(j, j + 1)], load_sem.at[group]).start()

    for copy in inputs:
        copy.wait()
    live = (lax.broadcasted_iota(jnp.int32, (32, 256), 1) < count_ref[0]).astype(F32)
    own_rows = pl.ds(pl.multiple_of(core * 16, 16), 16)
    sibling_rows = pl.ds(pl.multiple_of((1 - core) * 16, 16), 16)
    ysend[0:16, :] = y_ref[sibling_rows, :] * live[0:16]
    ysend[16:24, :] = live[0:8]
    r[:, mine] = y_ref[own_rows, :] * live[0:16]
    mask[:, mine] = live[0:8]
    q[...] = jnp.zeros_like(q)
    p[...] = jnp.zeros_like(p)
    w[...] = jnp.zeros_like(w)
    total[...] = jnp.zeros_like(total)

    lane = lax.broadcasted_iota(jnp.int32, (16, TILE), 1)
    sub = lax.broadcasted_iota(jnp.int32, (16, TILE), 0)
    eye = (lane == sub).astype(F32)
    field = lane // 16
    def ridge_of(which):
        pick = (lax.broadcasted_iota(jnp.int32, (16, 32), 1)
                == lax.broadcasted_iota(jnp.int32, (16, 32), 0) + which * 16).astype(F32)
        return jnp.sum(ridge_ref[...] * pick, axis=1, keepdims=True)

    ridge, ridge2 = ridge_of(core), ridge_of(1 - core)

    def to_row(column, which):
        return jnp.sum(column * which, axis=0, keepdims=True)

    def to_column(row, which):
        return jnp.sum(row * which, axis=1, keepdims=True)

    def lanes(v):
        out = add_up([v[:, j:j + TILE] for j in range(0, v.shape[1], TILE)])
        return jnp.sum(out, axis=1, keepdims=True)

    def pack(*columns):
        out = jnp.zeros((16, TILE), F32)
        for k, column in enumerate(columns):
            for place in range(3):
                head = column.astype(BF16).astype(F32)
                out = jnp.where(field == 3 * k + place, head, out)
                column = column - head
        return out.astype(BF16)

    def unpack(v):
        return [jnp.sum(jnp.where(field // 3 == k, v, 0.0), axis=1, keepdims=True) * 0.0625 for k in range(2)]

    def curvature(n):
        wait(drow.at[n, pl.ds(0, PEERS)], d_recv.at[n])
        return to_column(add_up([drow[n, j] for j in range(CHIPS)]), eye)

    def last_curvature(which):
        return to_column(add_up([dlast[which * CHIPS + j] for j in range(CHIPS)]), eye)

    def send_row(n, j):
        send(drow.at[n, me], drow.at[n, me], d_send, d_recv.at[n], peers[j])

    for group in range(FAR_GROUPS):
        wait(a.at[mine, slots(*GROUPS[group])], load_sem.at[group])
    for k, rows in enumerate((r[:, mine], ysend[0:16, :])):
        fsend[k] = jnp.dot(rows.astype(BF16), a[mine, slots(0, FAR)], preferred_element_type=F32).astype(BF16)

    pl.semaphore_wait(barrier, 2 * PEERS + NX)

    for group in range(FAR_GROUPS):
        for j in range(*GROUPS[group]):
            send(fsend.at[0, :, slots(j, j + 1)], trecv.at[0, j], t_send, t_recv.at[0, group], peers[j])
            send(fsend.at[1, :, slots(j, j + 1)], fextra.at[j], f_send, f_recv, cross_peers[j])

    y_copy = send(ysend, yrecv, y_sems.at[0], y_sems.at[1], sibling)
    pushes = {}
    for group in (*range(FAR_GROUPS, len(GROUPS)), *range(FAR_GROUPS)):
        part = a.at[mine, slots(*GROUPS[group])]
        if group >= FAR_GROUPS:
            wait(part, load_sem.at[group])
        pushes[group] = send(part, part, push_send.at[group], push_recv.at[group], sibling)
    y_copy.wait()
    r[:, others] = yrecv[0:16, :]
    mask[:, others] = yrecv[16:24, :]
    s[...] = r[...].astype(BF16)

    def step(n, carry):
        gamma, norm, guess, beta = carry
        first = n == 0
        inv_gamma, inv_guess = 1.0 / gamma, 1.0 / guess
        def scatter(group, lo, hi):
            part = jnp.dot(s[...], a[:, slots(lo, hi)], preferred_element_type=F32)
            tsend[n, :, slots(lo, hi)] = part.astype(BF16)
            for j in range(lo, min(hi, PEERS)):
                send(tsend.at[n, :, slots(j, j + 1)], trecv.at[n, j], t_send, t_recv.at[n, group], peers[j])
            return part

        for group, (lo, hi) in enumerate(GROUPS):
            if group < FAR_GROUPS:
                @pl.when(n > 0)
                def _():
                    scatter(group, lo, hi)
                continue

            @pl.when(n == 0)
            def _():
                pushes[group].wait_recv()
            part = scatter(group, lo, hi)
            if hi == CHIPS:
                summed = part[:, (PEERS - lo) * TILE:]
        rows = jnp.where(first, r[...], q[...])
        drow[n, me] = to_row(lanes(rows * rows), eye)
        for j in range(PEERS):
            send_row(n, j)

        @pl.when(n == 0)
        def _():
            for group in range(FAR_GROUPS):
                pushes[group].wait_recv()
            for lo, hi in GROUPS:
                at[slots(lo, hi), :] = a[:, slots(lo, hi)].T

        @pl.when(n > 0)
        def _():
            p[...] = g[...].astype(F32) + beta * p[...]

        summed = summed - ridge * (w[:, tile(me)] + guess * p[:, tile(me)])
        for group, (lo, hi) in reversed(list(enumerate(GROUPS))):
            hi = min(hi, PEERS)
            wait(trecv.at[n, pl.ds(lo, hi - lo)], t_recv.at[n, group])
            for j in range(lo, hi):
                summed = summed + trecv[n, j].astype(F32)
        @pl.when(n == 0)
        def _():
            wait(fextra, f_recv)
        extra = fextra[0].astype(F32)
        for j in range(1, FAR):
            extra = extra + fextra[j].astype(F32)
        summed = summed + jnp.where(first, extra, 0.0)
        ahead[n, :, tile(me)] = summed.astype(BF16)
        for group, (lo, hi) in enumerate(GROUPS):
            for j in range(lo, min(hi, PEERS)):
                part = ahead.at[n, :, tile(me)]
                send(part, part, g_send, g_recv.at[n, group], peers[j])

        energy = curvature(n)
        alpha = jnp.where(first, 0.0, gamma / (energy + ridge * norm))
        ratio = jnp.where(first, 1.0, alpha * inv_guess)
        r[...] = r[...] - alpha * q[...]
        w[...] = w[...] + alpha * p[...]
        keep = 1.0 - ratio

        image = jnp.zeros((16, 512), F32)
        for last in (LATE, *range(LATE + 1, len(GROUPS)))[::-1]:
            for group in range(LATE, -1, -1) if last == LATE else (last,):
                lo, hi = GROUPS[group]
                wait(ahead.at[n, :, slots(0, min(hi, PEERS) - lo)], g_recv.at[n, group])
            for j in reversed(range(0 if last == LATE else lo, GROUPS[last][1])):
                at_j = tile(chips[j])
                grad = keep * total[:, at_j] + ratio * ahead[n, :, at_j].astype(F32)
                total[:, at_j] = grad
                grad = grad.astype(BF16)
                g[:, at_j] = grad
                image = image + jnp.dot(grad, at[slots(j, j + 1), :], preferred_element_type=F32)
        grad = g[...].astype(F32)
        xbuf[n, x, :, 512:] = pack(lanes(grad * grad), lanes(grad * p[...]))
        xbuf[n, x, :, 0:512] = image.astype(BF16)
        for device in x_peers:
            send(xbuf.at[n, x], xbuf.at[n, x], x_send, x_recv.at[n], device)
        wait(xbuf.at[n, pl.ds(0, NX - 1)], x_recv.at[n])
        image = ((xbuf[n, 0].astype(F32) + xbuf[n, 1].astype(F32))
                 + (xbuf[n, 2].astype(F32) + xbuf[n, 3].astype(F32)))
        gamma_new, cross = unpack(image[:, 512:])
        beta = jnp.where(first, 0.0, gamma_new * inv_gamma)
        norm = gamma_new + 2.0 * beta * cross + beta * beta * norm
        guess = jnp.where(first, (2.0 / 3.0) * energy / gamma_new, 1.15 * alpha)
        fresh_q = image[:, 0:512] * mask[0:1, :] + beta * q[...]
        q[...] = fresh_q
        s[...] = (r[...] - guess * fresh_q).astype(BF16)
        return gamma_new, norm, guess, beta

    one = jnp.ones((16, 1), F32)
    gamma, norm, guess, beta = lax.fori_loop(0, ITERS, step, (one, one, one, one))

    drow[ITERS, me] = to_row(lanes(q[...] * q[...]), eye)
    for j in range(PEERS):
        for device in (peers[j], cross_peers[j]):
            send(drow.at[ITERS, me], dlast.at[core * CHIPS + me], dl_send, dl_recv, device)
    send(drow.at[ITERS, me], dlast.at[core * CHIPS + me], dl_send, dl_recv, sibling)
    dlast[core * CHIPS + me] = drow[ITERS, me]
    state_out[0] = jnp.broadcast_to(gamma, (16, TILE))
    state_out[1] = jnp.broadcast_to(norm, (16, TILE))
    send(state_out, state_in, pub_send.at[0], pub_recv.at[0], sibling)
    send(w, w2, pub_send.at[1], pub_recv.at[1], sibling)
    send(r.at[:, others], r2, pub_send.at[2], pub_recv.at[2], sibling)
    send(q.at[:, others], q2, pub_send.at[3], pub_recv.at[3], sibling)
    p[...] = g[...].astype(F32) + beta * p[...]
    send(p, p2, pub_send.at[4], pub_recv.at[4], sibling)
    for k, ref in enumerate((state_in, w2, r2, q2, p2)):
        wait(ref, pub_recv.at[k])
        wait(ref, pub_send.at[k])
    wait(dlast.at[pl.ds(0, 2 * CHIPS - 1)], dl_recv)
    alpha = gamma / (last_curvature(core) + ridge * norm)
    alpha2 = state_in[0, :, 0:1] / (last_curvature(1 - core) + ridge2 * state_in[1, :, 0:1])
    w[...] = w[...] + alpha * p[...]
    w2[...] = w2[...] + alpha2 * p2[...]
    r[:, mine] = r[:, mine] - alpha * q[:, mine]
    r2[...] = r2[...] - alpha2 * q2[...]
    outs = [pltpu.make_async_copy(src, dst, pub_local.at[k]) for k, (src, dst) in enumerate((
        (w, w_out.at[own_rows]), (w2, w_out.at[sibling_rows]),
        (r.at[:, mine], r_out.at[own_rows]), (r2, r_out.at[sibling_rows])))]
    for copy in outs:
        copy.start()
    for copy in outs:
        copy.wait()
    for push in pushes.values():
        push.wait_send()
    wait(fextra, f_send)
    wait(tsend.at[:, :, slots(0, PEERS)], t_send)
    wait(ahead.at[:, :, slots(0, PEERS)], g_send)
    wait(drow.at[pl.ds(0, ITERS), pl.ds(0, PEERS)], d_send)
    wait(dlast.at[pl.ds(0, 2 * CHIPS - 1)], dl_send)
    wait(xbuf.at[:, pl.ds(0, NX - 1)], x_send)


def hand_over(w_in, r_in, w_out, r_out, w, r, sems):
    parts = [(r_in, r, r_out)] + [
        (w_in.at[rows], w.at[rows], w_out.at[rows]) for rows in (pl.ds(8 * k, 8) for k in range(4))]
    loads = [pltpu.make_async_copy(src, at, sems.at[0, k]) for k, (src, at, _) in enumerate(parts)]
    stores = [pltpu.make_async_copy(at, dst, sems.at[1, k]) for k, (_, at, dst) in enumerate(parts)]
    for load in loads:
        load.start()
    for load, store in zip(loads, stores):
        load.wait()
        store.start()
    for store in stores:
        store.wait()


def local(activations, targets, counts, ridge):
    any_ = pl.BlockSpec(memory_space=pl.ANY)
    hbm = pl.BlockSpec(memory_space=pltpu.HBM)
    dma = pltpu.SemaphoreType.DMA
    groups = len(GROUPS)
    w, r = pl.pallas_call(
        kernel,
        out_shape=[jax.ShapeDtypeStruct((32, n), F32) for n in (4096, 256)],
        in_specs=[hbm] * 4,
        out_specs=[any_] * 2,
        scratch_shapes=[
            pltpu.VMEM((32, 256), F32),
            pltpu.SMEM((1,), jnp.int32),
            pltpu.VMEM((1, 32), F32),
            dma((3,)),
            pltpu.VMEM((512, 4096), BF16),
            pltpu.VMEM((4096, 512), BF16),
            pltpu.VMEM((24, 256), F32),
            pltpu.VMEM((24, 256), F32),
            pltpu.VMEM((8, 512), F32),
            pltpu.VMEM((16, 512), F32),
            pltpu.VMEM((16, 512), F32),
            pltpu.VMEM((16, 512), BF16),
            pltpu.VMEM((16, 4096), F32),
            pltpu.VMEM((16, 4096), F32),
            pltpu.VMEM((16, 4096), F32),
            pltpu.VMEM((ITERS, 16, 4096), BF16),
            pltpu.VMEM((ITERS, PEERS, 16, TILE), BF16),
            pltpu.VMEM((2, 16, FAR * TILE), BF16),
            pltpu.VMEM((FAR, 16, TILE), BF16),
            pltpu.VMEM((ITERS + 1, CHIPS, 1, TILE), F32),
            pltpu.VMEM((ITERS, 16, 4096), BF16),
            pltpu.VMEM((16, 4096), BF16),
            pltpu.VMEM((ITERS, NX, 16, 512 + TILE), BF16),
            pltpu.VMEM((2 * CHIPS, 1, TILE), F32),
            pltpu.VMEM((2, 16, TILE), F32),
            pltpu.VMEM((2, 16, TILE), F32),
            pltpu.VMEM((16, 4096), F32),
            pltpu.VMEM((16, 4096), F32),
            pltpu.VMEM((16, 256), F32),
            pltpu.VMEM((16, 256), F32),
            dma((groups,)), dma((groups,)), dma((groups,)), dma((2,)),
            dma, dma((ITERS, groups)), dma, dma, dma, dma((ITERS + 1,)),
            dma, dma((ITERS, groups)), dma, dma((ITERS,)), dma, dma,
            dma((5,)), dma((5,)), dma((5,)),
        ],
        compiler_params=pltpu.CompilerParams(
            collective_id=0, has_side_effects=True, vmem_limit_bytes=58 * 2**20),
        name="cgls",
    )(activations, targets.T, counts, ridge[None, :])
    w, r = pl.pallas_call(
        hand_over,
        out_shape=[jax.ShapeDtypeStruct((32, n), F32) for n in (4096, 256)],
        in_specs=[hbm] * 2,
        out_specs=[any_] * 2,
        scratch_shapes=[pltpu.VMEM((32, 4096), F32), pltpu.VMEM((32, 256), F32), dma((2, 5))],
        compiler_params=pltpu.CompilerParams(vmem_limit_bytes=58 * 2**20),
        name="hand_over",
    )(w, r)
    return w.T, r.T


def solution(mesh):
    placed = (P("tok", "feat"), P("tok", None), P("tok"), P())
    return jax.shard_map(
        local,
        mesh=mesh,
        in_specs=placed,
        out_specs=(P("feat", None), P("tok", None)),
        check_vma=False,
    )
```

```python
import jax
import jax.numpy as jnp
from jax import lax
from jax.experimental import pallas as pl
from jax.experimental.pallas import tpu as pltpu
from jax.sharding import PartitionSpec as P

ITERS = 4
NY, NZ, NX = 4, 8, 4
CHIPS = NY * NZ
MESH = pl.DeviceIdType.MESH
F32, BF16 = jnp.float32, jnp.bfloat16


def hops(offset):
    dy, dz = offset
    return min(dy, NY - dy) + min(dz, NZ - dz)


OFFSETS = sorted(((dy, dz) for dy in range(NY) for dz in range(NZ)), key=lambda o: (-hops(o), min(o[1], NZ - o[1]), o))
PEERS = CHIPS - 1
GROUPS = ((0, 1), (1, 5), (5, 12), (12, 20), (20, 27), (27, 32))
LATE = 1
FAR_GROUPS = 2
FAR = GROUPS[FAR_GROUPS - 1][1]
TILE = 128


def add_up(parts):
    while len(parts) > 1:
        parts = [sum(parts[i + 1:i + 2], parts[i]) for i in range(0, len(parts), 2)]
    return parts[0]


def kernel(a_hbm, y_hbm, count_hbm, ridge_hbm, w_out, r_out,
           y_ref, count_ref, ridge_ref, in_sems, a, at, ysend, yrecv, mask, r, q, s, p, w, total, tsend, trecv, fsend, fextra, drow, ahead, g, xbuf, dlast, state_out, state_in, w2, p2, r2, q2,
           load_sem, push_send, push_recv, y_sems, t_send, t_recv, f_send, f_recv, d_send, d_recv,
           g_send, g_recv, x_send, x_recv, dl_send, dl_recv, pub_local, pub_send, pub_recv):
    tok, x = lax.axis_index("tok"), lax.axis_index("feat")
    core = lax.rem(tok, 2)
    z, y = lax.rem(tok // 2, NZ), tok // (2 * NZ)
    chips = [lax.rem(y + dy, NY) * NZ + lax.rem(z + dz, NZ) for dy, dz in OFFSETS]
    me = chips[-1]
    mine = pl.ds(pl.multiple_of(core * 256, 256), 256)
    others = pl.ds(pl.multiple_of((1 - core) * 256, 256), 256)
    sibling = (me * 2 + 1 - core, x)
    peers = [(chip * 2 + core, x) for chip in chips[:PEERS]]
    cross_peers = [(chip * 2 + 1 - core, x) for chip in chips[:PEERS]]
    x_peers = [(tok, lax.rem(x + d, NX)) for d in (2, 1, 3)]

    def tile(chip):
        return pl.ds(pl.multiple_of(chip * TILE, TILE), TILE)

    def slots(lo, hi):
        return slice(lo * TILE, hi * TILE)

    def send(src, dst, send_sem, recv_sem, device):
        copy = pltpu.make_async_remote_copy(
            src_ref=src, dst_ref=dst, send_sem=send_sem, recv_sem=recv_sem,
            device_id=device, device_id_type=MESH)
        copy.start()
        return copy

    def wait(ref, sem):
        pltpu.make_async_copy(ref, ref, sem).wait()

    barrier = pltpu.get_barrier_semaphore()
    for device in peers + x_peers + [sibling] + cross_peers:
        pl.semaphore_signal(barrier, inc=1, device_id=device, device_id_type=MESH)

    inputs = [
        pltpu.make_async_copy(src, dst, in_sems.at[k])
        for k, (src, dst) in enumerate(((count_hbm, count_ref), (y_hbm, y_ref), (ridge_hbm, ridge_ref)))]
    for copy in inputs:
        copy.start()
    for group, (lo, hi) in enumerate(GROUPS):
        for j in range(lo, hi):
            pltpu.make_async_copy(
                a_hbm.at[:, tile(chips[j])], a.at[mine, slots(j, j + 1)], load_sem.at[group]).start()

    for copy in inputs:
        copy.wait()
    live = (lax.broadcasted_iota(jnp.int32, (32, 256), 1) < count_ref[0]).astype(F32)
    own_rows = pl.ds(pl.multiple_of(core * 16, 16), 16)
    sibling_rows = pl.ds(pl.multiple_of((1 - core) * 16, 16), 16)
    ysend[0:16, :] = y_ref[sibling_rows, :] * live[0:16]
    ysend[16:24, :] = live[0:8]
    r[:, mine] = y_ref[own_rows, :] * live[0:16]
    mask[:, mine] = live[0:8]
    q[...] = jnp.zeros_like(q)
    p[...] = jnp.zeros_like(p)
    w[...] = jnp.zeros_like(w)
    total[...] = jnp.zeros_like(total)

    lane = lax.broadcasted_iota(jnp.int32, (16, TILE), 1)
    sub = lax.broadcasted_iota(jnp.int32, (16, TILE), 0)
    eye = (lane == sub).astype(F32)
    field = lane // 16
    def ridge_of(which):
        pick = (lax.broadcasted_iota(jnp.int32, (16, 32), 1)
                == lax.broadcasted_iota(jnp.int32, (16, 32), 0) + which * 16).astype(F32)
        return jnp.sum(ridge_ref[...] * pick, axis=1, keepdims=True)

    ridge, ridge2 = ridge_of(core), ridge_of(1 - core)

    def to_row(column, which):
        return jnp.sum(column * which, axis=0, keepdims=True)

    def to_column(row, which):
        return jnp.sum(row * which, axis=1, keepdims=True)

    def lanes(v):
        out = add_up([v[:, j:j + TILE] for j in range(0, v.shape[1], TILE)])
        return jnp.sum(out, axis=1, keepdims=True)

    def pack(*columns):
        out = jnp.zeros((16, TILE), F32)
        for k, column in enumerate(columns):
            for place in range(3):
                head = column.astype(BF16).astype(F32)
                out = jnp.where(field == 3 * k + place, head, out)
                column = column - head
        return out.astype(BF16)

    def unpack(v):
        return [jnp.sum(jnp.where(field // 3 == k, v, 0.0), axis=1, keepdims=True) * 0.0625 for k in range(2)]

    def curvature(n):
        wait(drow.at[n, pl.ds(0, PEERS)], d_recv.at[n])
        return to_column(add_up([drow[n, j] for j in range(CHIPS)]), eye)

    def last_curvature(which):
        return to_column(add_up([dlast[which * CHIPS + j] for j in range(CHIPS)]), eye)

    def send_row(n, j):
        send(drow.at[n, me], drow.at[n, me], d_send, d_recv.at[n], peers[j])

    for group in range(FAR_GROUPS):
        wait(a.at[mine, slots(*GROUPS[group])], load_sem.at[group])
    for k, rows in enumerate((r[:, mine], ysend[0:16, :])):
        fsend[k] = jnp.dot(rows.astype(BF16), a[mine, slots(0, FAR)], preferred_element_type=F32).astype(BF16)

    pl.semaphore_wait(barrier, 2 * PEERS + NX)

    for group in range(FAR_GROUPS):
        for j in range(*GROUPS[group]):
            send(fsend.at[0, :, slots(j, j + 1)], trecv.at[0, j], t_send, t_recv.at[0, group], peers[j])
            send(fsend.at[1, :, slots(j, j + 1)], fextra.at[j], f_send, f_recv, cross_peers[j])

    y_copy = send(ysend, yrecv, y_sems.at[0], y_sems.at[1], sibling)
    pushes = {}
    for group in (*range(FAR_GROUPS, len(GROUPS)), *range(FAR_GROUPS)):
        part = a.at[mine, slots(*GROUPS[group])]
        if group >= FAR_GROUPS:
            wait(part, load_sem.at[group])
        pushes[group] = send(part, part, push_send.at[group], push_recv.at[group], sibling)
    y_copy.wait()
    r[:, others] = yrecv[0:16, :]
    mask[:, others] = yrecv[16:24, :]
    s[...] = r[...].astype(BF16)

    def step(n, carry):
        gamma, norm, guess, beta, alpha = carry
        first = n == 0
        inv_gamma, inv_guess = 1.0 / gamma, 1.0 / guess
        def scatter(group, lo, hi):
            part = jnp.dot(s[...], a[:, slots(lo, hi)], preferred_element_type=F32)
            tsend[n, :, slots(lo, hi)] = part.astype(BF16)
            for j in range(lo, min(hi, PEERS)):
                send(tsend.at[n, :, slots(j, j + 1)], trecv.at[n, j], t_send, t_recv.at[n, group], peers[j])
            return part

        for group, (lo, hi) in enumerate(GROUPS):
            if group < FAR_GROUPS:
                @pl.when(n > 0)
                def _():
                    scatter(group, lo, hi)
                continue

            @pl.when(n == 0)
            def _():
                pushes[group].wait_recv()
            part = scatter(group, lo, hi)
            if hi == CHIPS:
                summed = part[:, (PEERS - lo) * TILE:]
        rows = jnp.where(first, r[...], q[...])
        drow[n, me] = to_row(lanes(rows * rows), eye)
        for j in range(PEERS):
            send_row(n, j)

        @pl.when(n == 0)
        def _():
            for group in range(FAR_GROUPS):
                pushes[group].wait_recv()
            for lo, hi in GROUPS:
                at[slots(lo, hi), :] = a[:, slots(lo, hi)].T

        @pl.when(n > 0)
        def _():
            w[...] = w[...] + alpha * p[...]
            p[...] = g[...].astype(F32) + beta * p[...]

        summed = summed - ridge * (w[:, tile(me)] + guess * p[:, tile(me)])
        for group, (lo, hi) in reversed(list(enumerate(GROUPS))):
            hi = min(hi, PEERS)
            if group == 0:
                @pl.when(n == 0)
                def _():
                    wait(fextra, f_recv)
                extra = add_up([fextra[j].astype(F32) for j in range(FAR)])
                summed = summed + jnp.where(first, extra, 0.0)
            wait(trecv.at[n, pl.ds(lo, hi - lo)], t_recv.at[n, group])
            for j in range(lo, hi):
                summed = summed + trecv[n, j].astype(F32)
        ahead[n, :, tile(me)] = summed.astype(BF16)
        for group, (lo, hi) in enumerate(GROUPS):
            for j in range(lo, min(hi, PEERS)):
                part = ahead.at[n, :, tile(me)]
                send(part, part, g_send, g_recv.at[n, group], peers[j])

        energy = curvature(n)
        alpha = jnp.where(first, 0.0, gamma / (energy + ridge * norm))
        ratio = jnp.where(first, 1.0, alpha * inv_guess)
        r[...] = r[...] - alpha * q[...]
        keep = 1.0 - ratio

        image = jnp.zeros((16, 512), F32)
        for last in (LATE, *range(LATE + 1, len(GROUPS)))[::-1]:
            for group in range(LATE, -1, -1) if last == LATE else (last,):
                lo, hi = GROUPS[group]
                wait(ahead.at[n, :, slots(0, min(hi, PEERS) - lo)], g_recv.at[n, group])
            for j in reversed(range(0 if last == LATE else lo, GROUPS[last][1])):
                at_j = tile(chips[j])
                grad = keep * total[:, at_j] + ratio * ahead[n, :, at_j].astype(F32)
                total[:, at_j] = grad
                grad = grad.astype(BF16)
                g[:, at_j] = grad
                image = image + jnp.dot(grad, at[slots(j, j + 1), :], preferred_element_type=F32)
        grad = g[...].astype(F32)
        xbuf[n, x, :, 512:] = pack(lanes(grad * grad), lanes(grad * p[...]))
        xbuf[n, x, :, 0:512] = image.astype(BF16)
        for device in x_peers:
            send(xbuf.at[n, x], xbuf.at[n, x], x_send, x_recv.at[n], device)
        wait(xbuf.at[n, pl.ds(0, NX - 1)], x_recv.at[n])
        image = ((xbuf[n, 0].astype(F32) + xbuf[n, 1].astype(F32))
                 + (xbuf[n, 2].astype(F32) + xbuf[n, 3].astype(F32)))
        gamma_new, cross = unpack(image[:, 512:])
        beta = jnp.where(first, 0.0, gamma_new * inv_gamma)
        norm = gamma_new + 2.0 * beta * cross + beta * beta * norm
        guess = jnp.where(first, (2.0 / 3.0) * energy / gamma_new, 1.15 * alpha)
        fresh_q = image[:, 0:512] * mask[0:1, :] + beta * q[...]
        q[...] = fresh_q
        s[...] = (r[...] - guess * fresh_q).astype(BF16)
        return gamma_new, norm, guess, beta, alpha

    one = jnp.ones((16, 1), F32)
    gamma, norm, guess, beta, alpha = lax.fori_loop(0, ITERS, step, (one,) * 5)

    drow[ITERS, me] = to_row(lanes(q[...] * q[...]), eye)
    for j in range(PEERS):
        for device in (peers[j], cross_peers[j]):
            send(drow.at[ITERS, me], dlast.at[core * CHIPS + me], dl_send, dl_recv, device)
    send(drow.at[ITERS, me], dlast.at[core * CHIPS + me], dl_send, dl_recv, sibling)
    dlast[core * CHIPS + me] = drow[ITERS, me]
    state_out[0] = jnp.broadcast_to(gamma, (16, TILE))
    state_out[1] = jnp.broadcast_to(norm, (16, TILE))
    send(state_out, state_in, pub_send.at[0], pub_recv.at[0], sibling)
    w[...] = w[...] + alpha * p[...]
    send(w, w2, pub_send.at[1], pub_recv.at[1], sibling)
    send(r.at[:, others], r2, pub_send.at[2], pub_recv.at[2], sibling)
    send(q.at[:, others], q2, pub_send.at[3], pub_recv.at[3], sibling)
    p[...] = g[...].astype(F32) + beta * p[...]
    send(p, p2, pub_send.at[4], pub_recv.at[4], sibling)
    for k, ref in enumerate((state_in, w2, r2, q2, p2)):
        wait(ref, pub_recv.at[k])
        wait(ref, pub_send.at[k])
    wait(dlast.at[pl.ds(0, 2 * CHIPS - 1)], dl_recv)
    alpha = gamma / (last_curvature(core) + ridge * norm)
    alpha2 = state_in[0, :, 0:1] / (last_curvature(1 - core) + ridge2 * state_in[1, :, 0:1])
    w[...] = w[...] + alpha * p[...]
    w2[...] = w2[...] + alpha2 * p2[...]
    r[:, mine] = r[:, mine] - alpha * q[:, mine]
    r2[...] = r2[...] - alpha2 * q2[...]
    outs = [pltpu.make_async_copy(src, dst, pub_local.at[k]) for k, (src, dst) in enumerate((
        (w, w_out.at[own_rows]), (w2, w_out.at[sibling_rows]),
        (r.at[:, mine], r_out.at[own_rows]), (r2, r_out.at[sibling_rows])))]
    for copy in outs:
        copy.start()
    for copy in outs:
        copy.wait()
    for push in pushes.values():
        push.wait_send()
    wait(fextra, f_send)
    wait(tsend.at[:, :, slots(0, PEERS)], t_send)
    wait(ahead.at[:, :, slots(0, PEERS)], g_send)
    wait(drow.at[pl.ds(0, ITERS), pl.ds(0, PEERS)], d_send)
    wait(dlast.at[pl.ds(0, 2 * CHIPS - 1)], dl_send)
    wait(xbuf.at[:, pl.ds(0, NX - 1)], x_send)


def hand_over(w_in, r_in, w_out, r_out, w, r, sems):
    parts = [(r_in, r, r_out)] + [
        (w_in.at[rows], w.at[rows], w_out.at[rows]) for rows in (pl.ds(8 * k, 8) for k in range(4))]
    loads = [pltpu.make_async_copy(src, at, sems.at[0, k]) for k, (src, at, _) in enumerate(parts)]
    stores = [pltpu.make_async_copy(at, dst, sems.at[1, k]) for k, (_, at, dst) in enumerate(parts)]
    for load in loads:
        load.start()
    for load, store in zip(loads, stores):
        load.wait()
        store.start()
    for store in stores:
        store.wait()


def local(activations, targets, counts, ridge):
    any_ = pl.BlockSpec(memory_space=pl.ANY)
    hbm = pl.BlockSpec(memory_space=pltpu.HBM)
    dma = pltpu.SemaphoreType.DMA
    groups = len(GROUPS)
    w, r = pl.pallas_call(
        kernel,
        out_shape=[jax.ShapeDtypeStruct((32, n), F32) for n in (4096, 256)],
        in_specs=[hbm] * 4,
        out_specs=[any_] * 2,
        scratch_shapes=[
            pltpu.VMEM((32, 256), F32),
            pltpu.SMEM((1,), jnp.int32),
            pltpu.VMEM((1, 32), F32),
            dma((3,)),
            pltpu.VMEM((512, 4096), BF16),
            pltpu.VMEM((4096, 512), BF16),
            pltpu.VMEM((24, 256), F32),
            pltpu.VMEM((24, 256), F32),
            pltpu.VMEM((8, 512), F32),
            pltpu.VMEM((16, 512), F32),
            pltpu.VMEM((16, 512), F32),
            pltpu.VMEM((16, 512), BF16),
            pltpu.VMEM((16, 4096), F32),
            pltpu.VMEM((16, 4096), F32),
            pltpu.VMEM((16, 4096), F32),
            pltpu.VMEM((ITERS, 16, 4096), BF16),
            pltpu.VMEM((ITERS, PEERS, 16, TILE), BF16),
            pltpu.VMEM((2, 16, FAR * TILE), BF16),
            pltpu.VMEM((FAR, 16, TILE), BF16),
            pltpu.VMEM((ITERS + 1, CHIPS, 1, TILE), F32),
            pltpu.VMEM((ITERS, 16, 4096), BF16),
            pltpu.VMEM((16, 4096), BF16),
            pltpu.VMEM((ITERS, NX, 16, 512 + TILE), BF16),
            pltpu.VMEM((2 * CHIPS, 1, TILE), F32),
            pltpu.VMEM((2, 16, TILE), F32),
            pltpu.VMEM((2, 16, TILE), F32),
            pltpu.VMEM((16, 4096), F32),
            pltpu.VMEM((16, 4096), F32),
            pltpu.VMEM((16, 256), F32),
            pltpu.VMEM((16, 256), F32),
            dma((groups,)), dma((groups,)), dma((groups,)), dma((2,)),
            dma, dma((ITERS, groups)), dma, dma, dma, dma((ITERS + 1,)),
            dma, dma((ITERS, groups)), dma, dma((ITERS,)), dma, dma,
            dma((5,)), dma((5,)), dma((5,)),
        ],
        compiler_params=pltpu.CompilerParams(
            collective_id=0, has_side_effects=True, vmem_limit_bytes=58 * 2**20),
        name="cgls",
    )(activations, targets.T, counts, ridge[None, :])
    w, r = pl.pallas_call(
        hand_over,
        out_shape=[jax.ShapeDtypeStruct((32, n), F32) for n in (4096, 256)],
        in_specs=[hbm] * 2,
        out_specs=[any_] * 2,
        scratch_shapes=[pltpu.VMEM((32, 4096), F32), pltpu.VMEM((32, 256), F32), dma((2, 5))],
        compiler_params=pltpu.CompilerParams(vmem_limit_bytes=58 * 2**20),
        name="hand_over",
    )(w, r)
    return w.T, r.T


def solution(mesh):
    placed = (P("tok", "feat"), P("tok", None), P("tok"), P())
    return jax.shard_map(
        local,
        mesh=mesh,
        in_specs=placed,
        out_specs=(P("feat", None), P("tok", None)),
        check_vma=False,
    )
```

```python
import jax
import jax.numpy as jnp
from jax import lax
from jax.experimental import pallas as pl
from jax.experimental.pallas import tpu as pltpu
from jax.sharding import PartitionSpec as P

ITERS = 4
NY, NZ, NX = 4, 8, 4
CHIPS = NY * NZ
MESH = pl.DeviceIdType.MESH
F32, BF16 = jnp.float32, jnp.bfloat16


def hops(offset):
    dy, dz = offset
    return min(dy, NY - dy) + min(dz, NZ - dz)


OFFSETS = sorted(((dy, dz) for dy in range(NY) for dz in range(NZ)), key=lambda o: (-hops(o), min(o[1], NZ - o[1]), o))
PEERS = CHIPS - 1
GROUPS = ((0, 1), (1, 5), (5, 12), (12, 20), (20, 27), (27, 32))
LATE = 0
FAR_GROUPS = 2
FAR = GROUPS[FAR_GROUPS - 1][1]
TILE = 128


def add_up(parts):
    while len(parts) > 1:
        parts = [sum(parts[i + 1:i + 2], parts[i]) for i in range(0, len(parts), 2)]
    return parts[0]


def kernel(a_hbm, y_hbm, count_hbm, ridge_hbm, w_out, r_out,
           y_ref, count_ref, ridge_ref, in_sems, a, at, ysend, yrecv, mask, r, q, s, p, w, total, tsend, trecv, fsend, fextra, drow, ahead, g, xbuf, dlast, state_out, state_in, w2, p2, r2, q2,
           load_sem, push_send, push_recv, y_sems, t_send, t_recv, f_send, f_recv, d_send, d_recv,
           g_send, g_recv, x_send, x_recv, dl_send, dl_recv, pub_local, pub_send, pub_recv):
    tok, x = lax.axis_index("tok"), lax.axis_index("feat")
    core = lax.rem(tok, 2)
    z, y = lax.rem(tok // 2, NZ), tok // (2 * NZ)
    chips = [lax.rem(y + dy, NY) * NZ + lax.rem(z + dz, NZ) for dy, dz in OFFSETS]
    me = chips[-1]
    mine = pl.ds(pl.multiple_of(core * 256, 256), 256)
    others = pl.ds(pl.multiple_of((1 - core) * 256, 256), 256)
    sibling = (me * 2 + 1 - core, x)
    peers = [(chip * 2 + core, x) for chip in chips[:PEERS]]
    cross_peers = [(chip * 2 + 1 - core, x) for chip in chips[:PEERS]]
    x_peers = [(tok, lax.rem(x + d, NX)) for d in (2, 1, 3)]

    def tile(chip):
        return pl.ds(pl.multiple_of(chip * TILE, TILE), TILE)

    def slots(lo, hi):
        return slice(lo * TILE, hi * TILE)

    def send(src, dst, send_sem, recv_sem, device):
        copy = pltpu.make_async_remote_copy(
            src_ref=src, dst_ref=dst, send_sem=send_sem, recv_sem=recv_sem,
            device_id=device, device_id_type=MESH)
        copy.start()
        return copy

    def wait(ref, sem):
        pltpu.make_async_copy(ref, ref, sem).wait()

    barrier = pltpu.get_barrier_semaphore()
    for device in peers + x_peers + [sibling] + cross_peers:
        pl.semaphore_signal(barrier, inc=1, device_id=device, device_id_type=MESH)

    inputs = [
        pltpu.make_async_copy(src, dst, in_sems.at[k])
        for k, (src, dst) in enumerate(((count_hbm, count_ref), (y_hbm, y_ref), (ridge_hbm, ridge_ref)))]
    for copy in inputs:
        copy.start()
    for group, (lo, hi) in enumerate(GROUPS):
        for j in range(lo, hi):
            pltpu.make_async_copy(
                a_hbm.at[:, tile(chips[j])], a.at[mine, slots(j, j + 1)], load_sem.at[group]).start()

    for copy in inputs:
        copy.wait()
    live = (lax.broadcasted_iota(jnp.int32, (32, 256), 1) < count_ref[0]).astype(F32)
    own_rows = pl.ds(pl.multiple_of(core * 16, 16), 16)
    sibling_rows = pl.ds(pl.multiple_of((1 - core) * 16, 16), 16)
    ysend[0:16, :] = y_ref[sibling_rows, :] * live[0:16]
    ysend[16:24, :] = live[0:8]
    r[:, mine] = y_ref[own_rows, :] * live[0:16]
    mask[:, mine] = live[0:8]
    q[...] = jnp.zeros_like(q)
    p[...] = jnp.zeros_like(p)
    w[...] = jnp.zeros_like(w)
    total[...] = jnp.zeros_like(total)

    lane = lax.broadcasted_iota(jnp.int32, (16, TILE), 1)
    sub = lax.broadcasted_iota(jnp.int32, (16, TILE), 0)
    eye = (lane == sub).astype(F32)
    field = lane // 16
    def ridge_of(which):
        pick = (lax.broadcasted_iota(jnp.int32, (16, 32), 1)
                == lax.broadcasted_iota(jnp.int32, (16, 32), 0) + which * 16).astype(F32)
        return jnp.sum(ridge_ref[...] * pick, axis=1, keepdims=True)

    ridge, ridge2 = ridge_of(core), ridge_of(1 - core)

    def to_row(column, which):
        return jnp.sum(column * which, axis=0, keepdims=True)

    def to_column(row, which):
        return jnp.sum(row * which, axis=1, keepdims=True)

    def lanes(v):
        out = add_up([v[:, j:j + TILE] for j in range(0, v.shape[1], TILE)])
        return jnp.sum(out, axis=1, keepdims=True)

    def pack(*columns):
        out = jnp.zeros((16, TILE), F32)
        for k, column in enumerate(columns):
            for place in range(3):
                head = column.astype(BF16).astype(F32)
                out = jnp.where(field == 3 * k + place, head, out)
                column = column - head
        return out.astype(BF16)

    def unpack(v):
        return [jnp.sum(jnp.where(field // 3 == k, v, 0.0), axis=1, keepdims=True) * 0.0625 for k in range(2)]

    def curvature(n):
        wait(drow.at[n, pl.ds(0, PEERS)], d_recv.at[n])
        return to_column(add_up([drow[n, j] for j in range(CHIPS)]), eye)

    def last_curvature(which):
        return to_column(add_up([dlast[which * CHIPS + j] for j in range(CHIPS)]), eye)

    def send_row(n, j):
        send(drow.at[n, me], drow.at[n, me], d_send, d_recv.at[n], peers[j])

    for group in range(FAR_GROUPS):
        wait(a.at[mine, slots(*GROUPS[group])], load_sem.at[group])
    for k, rows in enumerate((r[:, mine], ysend[0:16, :])):
        fsend[k] = jnp.dot(rows.astype(BF16), a[mine, slots(0, FAR)], preferred_element_type=F32).astype(BF16)

    pl.semaphore_wait(barrier, 2 * PEERS + NX)

    for group in range(FAR_GROUPS):
        for j in range(*GROUPS[group]):
            send(fsend.at[0, :, slots(j, j + 1)], trecv.at[0, j], t_send, t_recv.at[0, group], peers[j])
            send(fsend.at[1, :, slots(j, j + 1)], fextra.at[j], f_send, f_recv, cross_peers[j])

    y_copy = send(ysend, yrecv, y_sems.at[0], y_sems.at[1], sibling)
    pushes = {}
    for group in (*range(FAR_GROUPS, len(GROUPS)), *range(FAR_GROUPS)):
        part = a.at[mine, slots(*GROUPS[group])]
        if group >= FAR_GROUPS:
            wait(part, load_sem.at[group])
        pushes[group] = send(part, part, push_send.at[group], push_recv.at[group], sibling)
    y_copy.wait()
    r[:, others] = yrecv[0:16, :]
    mask[:, others] = yrecv[16:24, :]
    s[...] = r[...].astype(BF16)

    def step(n, carry):
        gamma, norm, guess, beta, alpha = carry
        first = n == 0
        inv_gamma, inv_guess = 1.0 / gamma, 1.0 / guess
        def scatter(group, lo, hi):
            part = jnp.dot(s[...], a[:, slots(lo, hi)], preferred_element_type=F32)
            tsend[n, :, slots(lo, hi)] = part.astype(BF16)
            for j in range(lo, min(hi, PEERS)):
                send(tsend.at[n, :, slots(j, j + 1)], trecv.at[n, j], t_send, t_recv.at[n, group], peers[j])
            return part

        for group, (lo, hi) in enumerate(GROUPS):
            if group < FAR_GROUPS:
                @pl.when(n > 0)
                def _():
                    scatter(group, lo, hi)
                continue

            @pl.when(n == 0)
            def _():
                pushes[group].wait_recv()
            part = scatter(group, lo, hi)
            if hi == CHIPS:
                summed = part[:, (PEERS - lo) * TILE:]
        rows = jnp.where(first, r[...], q[...])
        drow[n, me] = to_row(lanes(rows * rows), eye)
        for j in range(PEERS):
            send_row(n, j)

        @pl.when(n == 0)
        def _():
            for group in range(FAR_GROUPS):
                pushes[group].wait_recv()
            for lo, hi in GROUPS:
                at[slots(lo, hi), :] = a[:, slots(lo, hi)].T

        @pl.when(n > 0)
        def _():
            w[...] = w[...] + alpha * p[...]
            p[...] = g[...].astype(F32) + beta * p[...]

        summed = summed - ridge * (w[:, tile(me)] + guess * p[:, tile(me)])
        for group, (lo, hi) in reversed(list(enumerate(GROUPS))):
            hi = min(hi, PEERS)
            if group == 0:
                @pl.when(n == 0)
                def _():
                    wait(fextra, f_recv)
                extra = add_up([fextra[j].astype(F32) for j in range(FAR)])
                summed = summed + jnp.where(first, extra, 0.0)
            wait(trecv.at[n, pl.ds(lo, hi - lo)], t_recv.at[n, group])
            for j in range(lo, hi):
                summed = summed + trecv[n, j].astype(F32)
        ahead[n, :, tile(me)] = summed.astype(BF16)
        for group, (lo, hi) in enumerate(GROUPS):
            for j in range(lo, min(hi, PEERS)):
                part = ahead.at[n, :, tile(me)]
                send(part, part, g_send, g_recv.at[n, group], peers[j])

        energy = curvature(n)
        alpha = jnp.where(first, 0.0, gamma / (energy + ridge * norm))
        ratio = jnp.where(first, 1.0, alpha * inv_guess)
        r[...] = r[...] - alpha * q[...]
        keep = 1.0 - ratio

        image = jnp.zeros((16, 512), F32)
        for last in (LATE, *range(LATE + 1, len(GROUPS)))[::-1]:
            for group in range(LATE, -1, -1) if last == LATE else (last,):
                lo, hi = GROUPS[group]
                wait(ahead.at[n, :, slots(0, min(hi, PEERS) - lo)], g_recv.at[n, group])
            for j in reversed(range(0 if last == LATE else lo, GROUPS[last][1])):
                at_j = tile(chips[j])
                grad = keep * total[:, at_j] + ratio * ahead[n, :, at_j].astype(F32)
                total[:, at_j] = grad
                grad = grad.astype(BF16)
                g[:, at_j] = grad
                image = image + jnp.dot(grad, at[slots(j, j + 1), :], preferred_element_type=F32)
        grad = g[...].astype(F32)
        xbuf[n, x, :, 512:] = pack(lanes(grad * grad), lanes(grad * p[...]))
        xbuf[n, x, :, 0:512] = image.astype(BF16)
        for device in x_peers:
            send(xbuf.at[n, x], xbuf.at[n, x], x_send, x_recv.at[n], device)
        wait(xbuf.at[n, pl.ds(0, NX - 1)], x_recv.at[n])
        image = ((xbuf[n, 0].astype(F32) + xbuf[n, 1].astype(F32))
                 + (xbuf[n, 2].astype(F32) + xbuf[n, 3].astype(F32)))
        gamma_new, cross = unpack(image[:, 512:])
        beta = jnp.where(first, 0.0, gamma_new * inv_gamma)
        norm = gamma_new + 2.0 * beta * cross + beta * beta * norm
        guess = jnp.where(first, (2.0 / 3.0) * energy / gamma_new, 1.15 * alpha)
        fresh_q = image[:, 0:512] * mask[0:1, :] + beta * q[...]
        q[...] = fresh_q
        s[...] = (r[...] - guess * fresh_q).astype(BF16)
        return gamma_new, norm, guess, beta, alpha

    one = jnp.ones((16, 1), F32)
    gamma, norm, guess, beta, alpha = lax.fori_loop(0, ITERS, step, (one,) * 5)

    drow[ITERS, me] = to_row(lanes(q[...] * q[...]), eye)
    for j in range(PEERS):
        for device in (peers[j], cross_peers[j]):
            send(drow.at[ITERS, me], dlast.at[core * CHIPS + me], dl_send, dl_recv, device)
    send(drow.at[ITERS, me], dlast.at[core * CHIPS + me], dl_send, dl_recv, sibling)
    dlast[core * CHIPS + me] = drow[ITERS, me]
    state_out[0] = jnp.broadcast_to(gamma, (16, TILE))
    state_out[1] = jnp.broadcast_to(norm, (16, TILE))
    send(state_out, state_in, pub_send.at[0], pub_recv.at[0], sibling)
    w[...] = w[...] + alpha * p[...]
    send(w, w2, pub_send.at[1], pub_recv.at[1], sibling)
    send(r.at[:, others], r2, pub_send.at[2], pub_recv.at[2], sibling)
    send(q.at[:, others], q2, pub_send.at[3], pub_recv.at[3], sibling)
    p[...] = g[...].astype(F32) + beta * p[...]
    send(p, p2, pub_send.at[4], pub_recv.at[4], sibling)
    for k, ref in enumerate((state_in, w2, r2, q2, p2)):
        wait(ref, pub_recv.at[k])
        wait(ref, pub_send.at[k])
    wait(dlast.at[pl.ds(0, 2 * CHIPS - 1)], dl_recv)
    alpha = gamma / (last_curvature(core) + ridge * norm)
    alpha2 = state_in[0, :, 0:1] / (last_curvature(1 - core) + ridge2 * state_in[1, :, 0:1])
    w[...] = w[...] + alpha * p[...]
    w2[...] = w2[...] + alpha2 * p2[...]
    r[:, mine] = r[:, mine] - alpha * q[:, mine]
    r2[...] = r2[...] - alpha2 * q2[...]
    outs = [pltpu.make_async_copy(src, dst, pub_local.at[k]) for k, (src, dst) in enumerate((
        (w, w_out.at[own_rows]), (w2, w_out.at[sibling_rows]),
        (r.at[:, mine], r_out.at[own_rows]), (r2, r_out.at[sibling_rows])))]
    for copy in outs:
        copy.start()
    for copy in outs:
        copy.wait()
    for push in pushes.values():
        push.wait_send()
    wait(fextra, f_send)
    wait(tsend.at[:, :, slots(0, PEERS)], t_send)
    wait(ahead.at[:, :, slots(0, PEERS)], g_send)
    wait(drow.at[pl.ds(0, ITERS), pl.ds(0, PEERS)], d_send)
    wait(dlast.at[pl.ds(0, 2 * CHIPS - 1)], dl_send)
    wait(xbuf.at[:, pl.ds(0, NX - 1)], x_send)


def hand_over(w_in, r_in, w_out, r_out, w, r, sems):
    parts = [(r_in, r, r_out)] + [
        (w_in.at[rows], w.at[rows], w_out.at[rows]) for rows in (pl.ds(8 * k, 8) for k in range(4))]
    loads = [pltpu.make_async_copy(src, at, sems.at[0, k]) for k, (src, at, _) in enumerate(parts)]
    stores = [pltpu.make_async_copy(at, dst, sems.at[1, k]) for k, (_, at, dst) in enumerate(parts)]
    for load in loads:
        load.start()
    for load, store in zip(loads, stores):
        load.wait()
        store.start()
    for store in stores:
        store.wait()


def local(activations, targets, counts, ridge):
    any_ = pl.BlockSpec(memory_space=pl.ANY)
    hbm = pl.BlockSpec(memory_space=pltpu.HBM)
    dma = pltpu.SemaphoreType.DMA
    groups = len(GROUPS)
    w, r = pl.pallas_call(
        kernel,
        out_shape=[jax.ShapeDtypeStruct((32, n), F32) for n in (4096, 256)],
        in_specs=[hbm] * 4,
        out_specs=[any_] * 2,
        scratch_shapes=[
            pltpu.VMEM((32, 256), F32),
            pltpu.SMEM((1,), jnp.int32),
            pltpu.VMEM((1, 32), F32),
            dma((3,)),
            pltpu.VMEM((512, 4096), BF16),
            pltpu.VMEM((4096, 512), BF16),
            pltpu.VMEM((24, 256), F32),
            pltpu.VMEM((24, 256), F32),
            pltpu.VMEM((8, 512), F32),
            pltpu.VMEM((16, 512), F32),
            pltpu.VMEM((16, 512), F32),
            pltpu.VMEM((16, 512), BF16),
            pltpu.VMEM((16, 4096), F32),
            pltpu.VMEM((16, 4096), F32),
            pltpu.VMEM((16, 4096), F32),
            pltpu.VMEM((ITERS, 16, 4096), BF16),
            pltpu.VMEM((ITERS, PEERS, 16, TILE), BF16),
            pltpu.VMEM((2, 16, FAR * TILE), BF16),
            pltpu.VMEM((FAR, 16, TILE), BF16),
            pltpu.VMEM((ITERS + 1, CHIPS, 1, TILE), F32),
            pltpu.VMEM((ITERS, 16, 4096), BF16),
            pltpu.VMEM((16, 4096), BF16),
            pltpu.VMEM((ITERS, NX, 16, 512 + TILE), BF16),
            pltpu.VMEM((2 * CHIPS, 1, TILE), F32),
            pltpu.VMEM((2, 16, TILE), F32),
            pltpu.VMEM((2, 16, TILE), F32),
            pltpu.VMEM((16, 4096), F32),
            pltpu.VMEM((16, 4096), F32),
            pltpu.VMEM((16, 256), F32),
            pltpu.VMEM((16, 256), F32),
            dma((groups,)), dma((groups,)), dma((groups,)), dma((2,)),
            dma, dma((ITERS, groups)), dma, dma, dma, dma((ITERS + 1,)),
            dma, dma((ITERS, groups)), dma, dma((ITERS,)), dma, dma,
            dma((5,)), dma((5,)), dma((5,)),
        ],
        compiler_params=pltpu.CompilerParams(
            collective_id=0, has_side_effects=True, vmem_limit_bytes=58 * 2**20),
        name="cgls",
    )(activations, targets.T, counts, ridge[None, :])
    w, r = pl.pallas_call(
        hand_over,
        out_shape=[jax.ShapeDtypeStruct((32, n), F32) for n in (4096, 256)],
        in_specs=[hbm] * 2,
        out_specs=[any_] * 2,
        scratch_shapes=[pltpu.VMEM((32, 4096), F32), pltpu.VMEM((32, 256), F32), dma((2, 5))],
        compiler_params=pltpu.CompilerParams(vmem_limit_bytes=58 * 2**20),
        name="hand_over",
    )(w, r)
    return w.T, r.T


def solution(mesh):
    placed = (P("tok", "feat"), P("tok", None), P("tok"), P())
    return jax.shard_map(
        local,
        mesh=mesh,
        in_specs=placed,
        out_specs=(P("feat", None), P("tok", None)),
        check_vma=False,
    )
```
